128 devices in a mesh: row: 16 (over x, y_lo, core), col: 8 (over z, y_hi).
Axes of the slice: x: 4, y: 4 (y_hi: 2, y_lo: 2; y = y_hi * 2 + y_lo), z: 4, core: 2. Of those that a mesh axis runs over, the one named last changes fastest.
Arguments:
- amplitudes: bfloat16 [24576, 24576], P('col', 'row'), may hold values from -0.0390625 to 0.0390625
- cholesky: bfloat16 [24576, 1280], P(('row', 'col')), may hold values from -5 to 5
- occ_map: int32 [24576], replicated, may hold values from 0 to 47
- vir_map: int32 [24576], replicated, may hold values from 0 to 511
Outputs:
- new_amplitudes: bfloat16 [24576, 24576], P('col', 'row')
The draws below stay inside these ranges and needn't reach their ends.
All inputs are finite; a program needn't handle non-finite values.
Results may differ from the reference program's by a relative error of at most 0.0056.
Values may be sent and summed in bfloat16 or wider, within the bound.
A program may use at most 128 MiB of HBM per device.

```python
import jax
import jax.numpy as jnp
from jax import lax

M = 24576
NAUX = 1280
NOCC = 48
NVIR = 512


def place_ends(values, own_key, least, largest):
    dims = values.shape
    index_at = [jax.random.randint(jax.random.fold_in(own_key, axis), (), 0, dims[axis]) for axis in range(len(dims))]
    values = values.at[tuple(index_at)].set(least)
    longest = dims.index(max(dims))
    index_at[longest] = (index_at[longest] + 1) % dims[longest]
    return values.at[tuple(index_at)].set(largest)


def levels(rng, dims, split, smallest, largest):
    factor_of = 1.0
    for position, blocks in split:
        heights = jax.random.uniform(jax.random.fold_in(jax.random.fold_in(rng, 6), position), (blocks,), jnp.float32, smallest / len(split), largest / len(split))
        factor_of = factor_of * jnp.repeat(jnp.exp(heights), dims[position] // blocks).reshape((-1,) + (1,) * (len(dims) - 1 - position))
    return factor_of


def centred(stream_key, dims, scale, most, shards=(), dtype=jnp.bfloat16):
    array = jax.random.normal(stream_key, dims, jnp.float32) * scale
    if len(shards) > 0:
        array = levels(stream_key, dims, shards, -0.22, 0.18) * array
    return jnp.clip(array, min=-most, max=most).astype(dtype)


def setup_inputs(seed: int = 0) -> dict:
    seeds = jax.random.split(jax.random.key(seed), 5)
    return {
        "amplitudes": centred(seeds[0], (M, M), M ** -0.5, 0.0390625, ((0, 8), (1, 16))),
        "cholesky": centred(seeds[1], (M, NAUX), 0.35, 5.0, ((0, 128),)),
        "occ_map": place_ends(jax.random.randint(seeds[2], (M,), 0, NOCC), jax.random.fold_in(seeds[2], 1), 0, NOCC - 1).astype(jnp.int32),
        "vir_map": place_ends(jax.random.randint(seeds[3], (M,), 0, NVIR), jax.random.fold_in(seeds[3], 1), 0, NVIR - 1).astype(jnp.int32),
    }


def pair_gap(occ_map, vir_map):
    occ = occ_map.astype(jnp.float32)
    vir = vir_map.astype(jnp.float32)
    return 0.5 + 2.5 * jnp.sqrt(vir / NVIR) + (0.5 + 2.5 * occ / NOCC)

def reference(amplitudes, cholesky, occ_map, vir_map):
    dressed = (cholesky.astype(jnp.float32) + jnp.dot(amplitudes, cholesky, preferred_element_type=jnp.float32)).astype(jnp.bfloat16)
    gap = pair_gap(occ_map, vir_map)

    def one_block(args):
        rows, gap_rows = args
        cycle = lax.dot_general(rows, dressed, (((1,), (1,)), ((), ())), preferred_element_type=jnp.float32)
        return (-cycle / (gap_rows[:, None] + gap[None, :])).astype(jnp.bfloat16)
    blocks = lax.map(one_block, (dressed.reshape(8, M // 8, NAUX), gap.reshape(8, M // 8)))
    return blocks.reshape(M, M)
```

```python
import jax
import jax.numpy as jnp
from jax import lax
from jax.experimental import pallas as pl
from jax.experimental.pallas import tpu as pltpu
from jax.sharding import PartitionSpec as P

NOCC = 48
NVIR = 512
MESH = pl.DeviceIdType.MESH
BF16 = jnp.bfloat16
F32 = jnp.float32

CHUNKS = 5
ORDER = [
    ("a1", 0), ("a1", 1), ("a1", 2), ("ob1", 0), ("a1", 3), ("a1", 4), ("a2", 0), ("a2", 1),
    ("a2", 2), ("a3", 0), ("a3", 1), ("a3", 2), ("ob2", 0), ("m1", 0), ("m2", 0), ("m1", 1),
    ("b1", 0), ("m2", 1), ("b1", 1), ("m1", 2), ("m2", 2), ("b2", 0), ("b1", 2), ("a2", 3),
    ("b2", 1), ("a2", 4), ("b3", 0), ("a3", 3), ("b2", 2), ("fin", 0), ("a3", 4), ("b3", 1),
    ("m1", 3), ("m2", 3), ("t2", 0), ("b1", 3), ("fin", 1), ("b3", 2), ("m1", 4), ("m2", 4),
    ("d1", 0), ("t2", 1), ("b1", 4), ("b2", 3), ("fin", 2), ("d2", 0), ("b2", 4), ("d1", 1),
    ("t2", 2), ("c2", 0), ("c2", 1), ("c2", 2), ("b3", 3), ("d2", 1), ("d3", 0), ("b3", 4),
    ("fin", 3), ("d1", 2), ("d3", 1), ("fin", 4), ("c3", 0), ("t2", 3), ("c2", 3), ("d2", 2),
    ("t2", 4), ("c3", 1), ("c2", 4), ("c3", 2), ("d3", 2), ("c4", 0), ("d1", 3), ("w", 0),
    ("d2", 3), ("c3", 3), ("d1", 4), ("c4", 1), ("d2", 4), ("w", 1), ("d3", 3), ("c3", 4),
    ("c4", 2), ("d3", 4), ("w", 2), ("c4", 3), ("w", 3), ("c4", 4), ("w", 4),
]

COPIES = [
    "a1", "a2p", "a2m", "a3p", "a3m", "dd", "b1p", "b1m", "b2p", "b2m", "b3",
    "c1", "c2p", "c2m", "c3p", "c3m", "c4", "t1", "t2", "d1", "d2p", "d2m", "d3p", "d3m",
]


def pair_gap(occ_map, vir_map):
    occ = occ_map.astype(jnp.float32)
    vir = vir_map.astype(jnp.float32)
    return 0.5 + 2.5 * jnp.sqrt(vir / NVIR) + (0.5 + 2.5 * occ / NOCC)


def place(x, yl, k, z, yh):
    return x * 4 + yl * 2 + k, z * 2 + yh


def kernel(t_hbm, b_own, rows_out, cols_out, t_v, bg, p_send, p_own, sib, b1s, b1r, b2s, b2r,
           b3s, b3r, rows, cols, t1r, ob1r, ob2r, send_sem, recv_sem, local_sem):
    r, c = lax.axis_index("row"), lax.axis_index("col")
    x, yl, k = r // 4, (r // 2) % 2, r % 2
    z, yh = c // 2, c % 2
    n = CHUNKS
    s = b_own.shape[0]
    w = b_own.shape[1] // n
    half = 8 * s

    xp, xm = place((x + 1) % 4, yl, k, z, yh), place((x + 3) % 4, yl, k, z, yh)
    zp, zm = place(x, yl, k, (z + 1) % 4, yh), place(x, yl, k, (z + 3) % 4, yh)
    low, high = place(x, 1 - yl, k, z, yh), place(x, yl, k, z, 1 - yh)
    other = place(x, yl, 1 - k, z, yh)
    out_z, in_z = place(x, yl, k, (z + x) % 4, yh), place(x, yl, k, (z + 4 - x) % 4, yh)
    mirror_x = (z + 4 - x) % 4
    mirror = place(mirror_x, yh, k, z, yl)
    moves = x != 0
    mirrored = jnp.logical_or(mirror_x != x, yh != yl)

    barrier = pltpu.get_barrier_semaphore()
    for device in (xp, xm, zp, zm, low, high, other):
        pl.semaphore_signal(barrier, inc=1, device_id=device, device_id_type=MESH)

    @pl.when(moves)
    def _():
        for device in (out_z, in_z):
            pl.semaphore_signal(barrier, inc=1, device_id=device, device_id_type=MESH)

    @pl.when(mirrored)
    def _():
        pl.semaphore_signal(barrier, inc=1, device_id=mirror, device_id_type=MESH)

    t_copy = pltpu.make_async_copy(t_hbm, t_v, local_sem.at[2 * n])
    t_copy.start()

    pl.semaphore_wait(barrier, 7 + 2 * moves.astype(jnp.int32) + mirrored.astype(jnp.int32))

    def copy(name, j, src, dst, device):
        at = j * len(COPIES) + COPIES.index(name) if name in COPIES else n * len(COPIES) + j
        return pltpu.make_async_remote_copy(
            src_ref=src, dst_ref=dst, send_sem=send_sem.at[at], recv_sem=recv_sem.at[at],
            device_id=device, device_id_type=MESH,
        )

    def rows_of(block, count):
        return pl.ds(pl.multiple_of(block * s, s), count * s)

    def here(pos):
        return (pos + z) % 4

    sent = []
    waiting = {}

    def send(name, j, src, dst, device, when=None):
        one = copy(name, j, src, dst, device)
        if when is None:
            one.start()
        else:
            pl.when(when)(one.start)
        sent.append((one, when))
        waiting[name, j] = (one, when)

    def arrive(name, j):
        one, when = waiting.pop((name, j))
        if when is None:
            one.wait_recv()
        else:
            pl.when(when)(one.wait_recv)

    def pair_out(name, j, buf, at, p, plus, minus):
        view = buf.at[j, rows_of(at + 2 * p, 2)]
        send(name + "p", j, view, view, plus)
        send(name + "m", j, view, view, minus)

    def pass_on(name, j, buf, at, before, after, q, plus, minus):
        up = buf.at[j, rows_of(at + 2 * before + q, 1)]
        down = buf.at[j, rows_of(at + 2 * after + 1 - q, 1)]
        send(name + "p", j, up, up, plus)
        send(name + "m", j, down, down, minus)

    tile = 2 * s

    def dressed_part(j, start, store):
        def step(i, carry):
            t = t_v[pl.ds(pl.multiple_of(start + i * tile, tile), tile), :]
            store(i, jnp.dot(t, bg[j], preferred_element_type=F32))
            return carry
        lax.fori_loop(0, half // tile, step, 0)

    def partial(j, block, count):
        at = rows_of(block, count)
        return p_own[j % p_own.shape[0], at] + sib[j, at].astype(F32)

    done = {}

    def run(name, j):
        own_a = rows_of(2 * z + yh, 1)
        own_c = rows_of(8 * k + 2 * here(x) + yl, 1)
        if name == "ob1":
            send("ob1", 0, b_own, ob1r, mirror, mirrored)

            @pl.when(jnp.logical_not(mirrored))
            def _():
                ob1r[...] = b_own[...]
        elif name == "ob2":
            arrive("ob1", 0)
            send("ob2", 1, ob1r, ob2r, in_z, moves)

            @pl.when(jnp.logical_not(moves))
            def _():
                ob2r[...] = ob1r[...]
        elif name == "a1":
            bg[j, own_a] = b_own[:, j * w:(j + 1) * w]
            send("a1", j, b_own.at[:, pl.ds(j * w, w)], bg.at[j, own_a], high)
        elif name == "a2":
            arrive("a1", j)
            pair_out("a2", j, bg, 0, z, zp, zm)
        elif name == "a3":
            arrive("a2p", j)
            arrive("a2m", j)
            pass_on("a3", j, bg, 0, (z + 3) % 4, (z + 1) % 4, yh, zp, zm)
        elif name == "m1":
            arrive("a3p", j)
            arrive("a3m", j)
            if not done:
                t_copy.wait()
                done["t"] = True

            def store(i, value):
                p_send[j, pl.ds(pl.multiple_of(i * tile, tile), tile)] = value.astype(BF16)
            dressed_part(j, (1 - k) * half, store)
            send("dd", j, p_send.at[j], sib.at[j], other)
        elif name == "m2":
            def store(i, value):
                p_own[j % p_own.shape[0], pl.ds(pl.multiple_of(i * tile, tile), tile)] = value
            dressed_part(j, k * half, store)
        elif name == "b1":
            arrive("dd", j)
            far = here(x + 2)
            b1s[j, 0] = partial(j, 2 * far + yl, 1).astype(BF16)
            b1s[j, 1] = partial(j, 2 * far + 1 - yl, 1).astype(BF16)
            send("b1p", j, b1s.at[j, 0], b1r.at[j, 0], xp)
            send("b1m", j, b1s.at[j, 1], b1r.at[j, 1], xm)
        elif name == "b2":
            arrive("b1p", j)
            arrive("b1m", j)
            for side, (step, q) in enumerate(((1, yl), (3, 1 - yl))):
                to = here(x + step)
                b2s[j, side, rows_of(q, 1)] = (
                    partial(j, 2 * to + q, 1) + b1r[j, side].astype(F32)).astype(BF16)
                b2s[j, side, rows_of(1 - q, 1)] = partial(j, 2 * to + 1 - q, 1).astype(BF16)
            send("b2p", j, b2s.at[j, 0], b2r.at[j, 0], xp)
            send("b2m", j, b2s.at[j, 1], b2r.at[j, 1], xm)
        elif name == "b3":
            arrive("b2p", j)
            arrive("b2m", j)

            def total(q):
                at = rows_of(q, 1)
                return partial(j, 2 * here(x) + q, 1) + (
                    b2r[j, 0, at].astype(F32) + b2r[j, 1, at].astype(F32))
            b3s[j] = total(1 - yl).astype(BF16)
            send("b3", j, b3s.at[j], b3r.at[j], low)
            p_own[j % p_own.shape[0], rows_of(2 * here(x) + yl, 1)] = total(yl)
        elif name == "fin":
            if "b" not in done:
                arrive("ob2", 1)
                done["b"] = True
            arrive("b3", j)
            value = (p_own[j % p_own.shape[0], rows_of(2 * here(x) + yl, 1)] + b3r[j].astype(F32)
                     + ob2r[:, j * w:(j + 1) * w].astype(F32)).astype(BF16)
            rows[j, own_c] = value
            send("t1", j, rows.at[j, own_c], t1r.at[j], out_z, moves)
            send("c1", j, rows.at[j, own_c], rows.at[j, own_c], low)

            @pl.when(jnp.logical_not(moves))
            def _():
                t1r[j] = value
        elif name == "c2":
            arrive("c1", j)
            pair_out("c2", j, rows, 8 * k, here(x), xp, xm)
        elif name == "c3":
            arrive("c2p", j)
            arrive("c2m", j)
            pass_on("c3", j, rows, 8 * k, here(x + 3), here(x + 1), yl, xp, xm)
        elif name == "c4":
            arrive("c3p", j)
            arrive("c3m", j)
            mine = rows.at[j, rows_of(8 * k, 8)]
            send("c4", j, mine, mine, other)
        elif name == "t2":
            arrive("t1", j)
            at = rows_of(2 * z + yl, 1)
            send("t2", j, t1r.at[j], cols.at[j, at], mirror, mirrored)

            @pl.when(jnp.logical_not(mirrored))
            def _():
                cols[j, at] = t1r[j]
        elif name == "d1":
            arrive("t2", j)
            send("d1", j, cols.at[j, own_a], cols.at[j, own_a], high)
        elif name == "d2":
            arrive("d1", j)
            pair_out("d2", j, cols, 0, z, zp, zm)
        elif name == "d3":
            arrive("d2p", j)
            arrive("d2m", j)
            pass_on("d3", j, cols, 0, (z + 3) % 4, (z + 1) % 4, yh, zp, zm)
        elif name == "w":
            arrive("d3p", j)
            arrive("d3m", j)
            arrive("c4", j)
            at = pl.ds(j * w, w)
            pltpu.make_async_copy(rows.at[j], rows_out.at[:, at], local_sem.at[j]).start()
            pltpu.make_async_copy(cols.at[j], cols_out.at[:, at], local_sem.at[n + j]).start()

    for name, j in ORDER:
        run(name, j)
    for j in range(n):
        at = pl.ds(j * w, w)
        pltpu.make_async_copy(rows.at[j], rows_out.at[:, at], local_sem.at[j]).wait()
        pltpu.make_async_copy(cols.at[j], cols_out.at[:, at], local_sem.at[n + j]).wait()
    for one, when in sent:
        if when is None:
            one.wait_send()
        else:
            pl.when(when)(one.wait_send)


def gather_dressed(amplitudes, cholesky):
    height, width = amplitudes.shape
    s, naux = cholesky.shape
    n = CHUNKS
    w = naux // n
    half = 8 * s
    many = n * len(COPIES) + 2
    return pl.pallas_call(
        kernel,
        out_shape=(
            jax.ShapeDtypeStruct((height, naux), BF16),
            jax.ShapeDtypeStruct((width, naux), BF16),
        ),
        in_specs=[pl.BlockSpec(memory_space=pl.ANY), pl.BlockSpec(memory_space=pltpu.VMEM)],
        out_specs=(pl.BlockSpec(memory_space=pl.ANY), pl.BlockSpec(memory_space=pl.ANY)),
        scratch_shapes=[
            pltpu.VMEM((height, width), BF16),
            pltpu.VMEM((n, 8 * s, w), BF16),
            pltpu.VMEM((n, half, w), BF16),
            pltpu.VMEM((n, half, w), F32),
            pltpu.VMEM((n, half, w), BF16),
            pltpu.VMEM((n, 2, s, w), BF16),
            pltpu.VMEM((n, 2, s, w), BF16),
            pltpu.VMEM((n, 2, 2 * s, w), BF16),
            pltpu.VMEM((n, 2, 2 * s, w), BF16),
            pltpu.VMEM((n, s, w), BF16),
            pltpu.VMEM((n, s, w), BF16),
            pltpu.VMEM((n, 2 * half, w), BF16),
            pltpu.VMEM((n, 8 * s, w), BF16),
            pltpu.VMEM((n, s, w), BF16),
            pltpu.VMEM((s, naux), BF16),
            pltpu.VMEM((s, naux), BF16),
            pltpu.SemaphoreType.DMA((many,)),
            pltpu.SemaphoreType.DMA((many,)),
            pltpu.SemaphoreType.DMA((2 * n + 1,)),
        ],
        compiler_params=pltpu.CompilerParams(
            collective_id=0, has_side_effects=True, vmem_limit_bytes=62 * 2**20),
        cost_estimate=pl.CostEstimate(
            flops=2 * height * width * naux, bytes_accessed=2 * height * width, transcendentals=0),
    )(amplitudes, cholesky)


def body(amplitudes, cholesky, occ_map, vir_map):
    height, width = amplitudes.shape
    p_start = lax.axis_index("col") * height
    q_start = lax.axis_index("row") * width
    rows, cols = gather_dressed(amplitudes, cholesky)
    cycle = lax.dot_general(
        rows, cols, (((1,), (1,)), ((), ())), preferred_element_type=jnp.float32
    )
    gap_rows = pair_gap(
        lax.dynamic_slice_in_dim(occ_map, p_start, height, 0),
        lax.dynamic_slice_in_dim(vir_map, p_start, height, 0),
    )
    gap_cols = pair_gap(
        lax.dynamic_slice_in_dim(occ_map, q_start, width, 0),
        lax.dynamic_slice_in_dim(vir_map, q_start, width, 0),
    )
    return (-cycle / (gap_rows[:, None] + gap_cols[None, :])).astype(jnp.bfloat16)


def solution(mesh):
    return jax.shard_map(
        body,
        mesh=mesh,
        in_specs=(P("col", "row"), P(("row", "col"), None), P(), P()),
        out_specs=P("col", "row"),
        check_vma=False,
    )
```

```python
import jax
import jax.numpy as jnp
from jax import lax
from jax.experimental import pallas as pl
from jax.experimental.pallas import tpu as pltpu
from jax.sharding import PartitionSpec as P

NOCC = 48
NVIR = 512
MESH = pl.DeviceIdType.MESH
BF16 = jnp.bfloat16
F32 = jnp.float32

WIDTHS = [256, 256, 256, 256, 256]
OWN_SLOTS = 3
SEND_SLOTS = 2
GPARTS = 3
GTILE = 256
ORDER = [
    ("a1", 0), ("a1", 1), ("gap", 0), ("a1", 2), ("ob1", 0), ("a1", 3), ("a1", 4), ("a2", 0),
    ("a2", 1), ("a2", 2), ("a3", 0), ("a3", 1), ("a3", 2), ("ob2", 0), ("m1", 0), ("m2", 0),
    ("m1", 1), ("b1", 0), ("m1", 2), ("m2", 1), ("b1", 1), ("m2", 2), ("b2", 0), ("b1", 2),
    ("a2", 3), ("a2", 4), ("b2", 1), ("b3", 0), ("a3", 3), ("b2", 2), ("fin", 0), ("a3", 4),
    ("b3", 1), ("m1", 3), ("m2", 3), ("t2", 0), ("b1", 3), ("fin", 1), ("b3", 2), ("m1", 4),
    ("m2", 4), ("d1", 0), ("t2", 1), ("b1", 4), ("b2", 3), ("fin", 2), ("d2", 0), ("b2", 4),
    ("d1", 1), ("t2", 2), ("c2", 0), ("c2", 1), ("c2", 2), ("b3", 3), ("d2", 1), ("d3", 0),
    ("b3", 4), ("fin", 3), ("d1", 2), ("d3", 1), ("fin", 4), ("c3", 0), ("t2", 3), ("c2", 3),
    ("d2", 2), ("t2", 4), ("c3", 1), ("c2", 4), ("c3", 2), ("d3", 2), ("c4", 0), ("d1", 3),
    ("w", 0), ("g2", 0), ("g1", 0), ("g0", 0), ("d2", 3), ("c3", 3), ("d1", 4), ("c4", 1),
    ("d2", 4), ("w", 1), ("g2", 1), ("d3", 3), ("g1", 1), ("g0", 1), ("c3", 4), ("c4", 2),
    ("d3", 4), ("w", 2), ("g2", 2), ("c4", 3), ("g1", 2), ("c4", 4), ("g0", 2), ("w", 3),
    ("g2", 3), ("g1", 3), ("g0", 3), ("w", 4), ("g2", 4), ("g1", 4), ("g0", 4),
]

COPIES = [
    "a1", "a2p", "a2m", "a3p", "a3m", "dd", "b1p", "b1m", "b2p", "b2m", "b3",
    "c1", "c2p", "c2m", "c3p", "c3m", "c4", "t1", "t2", "d1", "d2p", "d2m", "d3p", "d3m",
]


def place(x, yl, k, z, yh):
    return x * 4 + yl * 2 + k, z * 2 + yh


def kernel(t_hbm, b_own, occ, vir, out, bg, p_send, p_own, sib, b1r, b2r, b3r, rows, cols, t1r,
           ob1r, ob2r, acc, gap, gap_rows, send_sem, recv_sem, local_sem):
    r, c = lax.axis_index("row"), lax.axis_index("col")
    x, yl, k = r // 4, (r // 2) % 2, r % 2
    z, yh = c // 2, c % 2
    n = len(WIDTHS)
    begin = [sum(WIDTHS[:j]) for j in range(n)]
    s = b_own.shape[0]
    half = 8 * s

    xp, xm = place((x + 1) % 4, yl, k, z, yh), place((x + 3) % 4, yl, k, z, yh)
    zp, zm = place(x, yl, k, (z + 1) % 4, yh), place(x, yl, k, (z + 3) % 4, yh)
    low, high = place(x, 1 - yl, k, z, yh), place(x, yl, k, z, 1 - yh)
    other = place(x, yl, 1 - k, z, yh)
    out_z, in_z = place(x, yl, k, (z + x) % 4, yh), place(x, yl, k, (z + 4 - x) % 4, yh)
    mirror_x = (z + 4 - x) % 4
    mirror = place(mirror_x, yh, k, z, yl)
    moves = x != 0
    mirrored = jnp.logical_or(mirror_x != x, yh != yl)

    barrier = pltpu.get_barrier_semaphore()
    for device in (xp, xm, zp, zm, low, high, other):
        pl.semaphore_signal(barrier, inc=1, device_id=device, device_id_type=MESH)

    @pl.when(moves)
    def _():
        for device in (out_z, in_z):
            pl.semaphore_signal(barrier, inc=1, device_id=device, device_id_type=MESH)

    @pl.when(mirrored)
    def _():
        pl.semaphore_signal(barrier, inc=1, device_id=mirror, device_id_type=MESH)

    t_copy = pltpu.make_async_copy(t_hbm, out, local_sem.at[0])
    t_copy.start()

    pl.semaphore_wait(barrier, 7 + 2 * moves.astype(jnp.int32) + mirrored.astype(jnp.int32))

    def copy(name, j, src, dst, device):
        at = j * len(COPIES) + COPIES.index(name) if name in COPIES else n * len(COPIES) + j
        return pltpu.make_async_remote_copy(
            src_ref=src, dst_ref=dst, send_sem=send_sem.at[at], recv_sem=recv_sem.at[at],
            device_id=device, device_id_type=MESH,
        )

    def rows_of(block, count):
        return pl.ds(pl.multiple_of(block * s, s), count * s)

    def here(pos):
        return (pos + z) % 4

    sent = {}
    waiting = {}

    def send(name, j, src, dst, device, when=None):
        one = copy(name, j, src, dst, device)
        if when is None:
            one.start()
        else:
            pl.when(when)(one.start)
        sent[name, j] = waiting[name, j] = (one, when)

    def arrive(name, j):
        one, when = waiting.pop((name, j))
        if when is None:
            one.wait_recv()
        else:
            pl.when(when)(one.wait_recv)

    def leave(name, j):
        one, when = sent.pop((name, j))
        if when is None:
            one.wait_send()
        else:
            pl.when(when)(one.wait_send)

    def pair_out(name, j, buf, at, p, plus, minus):
        view = buf.at[rows_of(at + 2 * p, 2)]
        send(name + "p", j, view, view, plus)
        send(name + "m", j, view, view, minus)

    def pass_on(name, j, buf, at, before, after, q, plus, minus):
        up = buf.at[rows_of(at + 2 * before + q, 1)]
        down = buf.at[rows_of(at + 2 * after + 1 - q, 1)]
        send(name + "p", j, up, up, plus)
        send(name + "m", j, down, down, minus)

    def dressed_part(j, start):
        t = out[pl.ds(pl.multiple_of(start, half), half), :]
        return jnp.dot(t, bg[j][...], preferred_element_type=F32)

    def own_of(j):
        return p_own[j % OWN_SLOTS].at[:, pl.ds(0, WIDTHS[j])]

    def partial(j, block, count):
        at = rows_of(block, count)
        return own_of(j)[at] + sib[j][at].astype(F32)

    def set_gaps():
        gap[...] = 0.5 + 2.5 * jnp.sqrt(vir[...].astype(F32) / NVIR) + (
            0.5 + 2.5 * occ[...].astype(F32) / NOCC)
        blocks = 2 * half // 128

        def turn(i, carry):
            line = gap[pl.ds(c * blocks + i, 1), :]
            gap_rows[pl.ds(pl.multiple_of(i * 128, 128), 128), :] = jnp.broadcast_to(line, (128, 128)).T
            return carry
        lax.fori_loop(0, blocks, turn, 0)

    def product(j, part):
        tiles = half // GTILE // GPARTS

        def step(i, carry):
            h = i // 2 + part * tiles
            top = pl.multiple_of(i % 2 * half, half)
            at = pl.multiple_of(h * GTILE, GTILE)
            value = lax.dot_general(
                rows[j][pl.ds(top, half), :], cols[j][pl.ds(at, GTILE), :],
                (((1,), (1,)), ((), ())), preferred_element_type=F32)
            where = pl.ds(top, half), pl.ds(at, GTILE)
            if j == 0:
                acc[where] = value
            elif j < n - 1:
                acc[where] += value
            else:
                value = acc[where] + value
                for lane in range(0, GTILE, 128):
                    line = gap[pl.ds(r * (half // 128) + h * (GTILE // 128) + lane // 128, 1), :]
                    both = gap_rows[pl.ds(top, half), :] + line
                    out[pl.ds(top, half), pl.ds(at + lane, 128)] = (
                        -value[:, lane:lane + 128] / both).astype(BF16)
            return carry
        lax.fori_loop(0, 2 * tiles, step, 0)

    done = {}

    def run(name, j):
        own_a = rows_of(2 * z + yh, 1)
        own_c = rows_of(8 * k + 2 * here(x) + yl, 1)
        w = WIDTHS[j]
        columns = pl.ds(begin[j], w)
        if name == "ob1":
            send("ob1", 0, b_own, ob1r, mirror, mirrored)

            @pl.when(jnp.logical_not(mirrored))
            def _():
                ob1r[...] = b_own[...]
        elif name == "ob2":
            arrive("ob1", 0)
            send("ob2", 1, ob1r, ob2r, in_z, moves)

            @pl.when(jnp.logical_not(moves))
            def _():
                ob2r[...] = ob1r[...]
        elif name == "gap":
            set_gaps()
        elif name == "a1":
            send("a1", j, b_own.at[:, columns], bg[j].at[own_a], high)
            bg[j][own_a] = b_own[:, columns]
        elif name == "a2":
            arrive("a1", j)
            pair_out("a2", j, bg[j], 0, z, zp, zm)
        elif name == "a3":
            arrive("a2p", j)
            arrive("a2m", j)
            pass_on("a3", j, bg[j], 0, (z + 3) % 4, (z + 1) % 4, yh, zp, zm)
        elif name == "m1":
            arrive("a3p", j)
            arrive("a3m", j)
            if "t" not in done:
                t_copy.wait()
                done["t"] = True
            if j >= SEND_SLOTS:
                leave("dd", j - SEND_SLOTS)
            slot = p_send[j % SEND_SLOTS].at[:, pl.ds(0, w)]
            slot[...] = dressed_part(j, (1 - k) * half).astype(BF16)
            send("dd", j, slot, sib[j], other)
        elif name == "m2":
            own_of(j)[...] = dressed_part(j, k * half)
        elif name == "b1":
            arrive("dd", j)
            for side, (q, device) in enumerate(((yl, xp), (1 - yl, xm))):
                block = 2 * here(x + 2) + q
                sib[j][rows_of(block, 1)] = partial(j, block, 1).astype(BF16)
                send("b1" + "pm"[side], j, sib[j].at[rows_of(block, 1)], b1r[j].at[side], device)
        elif name == "b2":
            arrive("b1p", j)
            arrive("b1m", j)
            for side, (step, q, device) in enumerate(((1, yl, xp), (3, 1 - yl, xm))):
                first = 2 * here(x + step)
                one, two = rows_of(first + q, 1), rows_of(first + 1 - q, 1)
                sib[j][one] = (partial(j, first + q, 1) + b1r[j][side].astype(F32)).astype(BF16)
                sib[j][two] = partial(j, first + 1 - q, 1).astype(BF16)
                send("b2" + "pm"[side], j, sib[j].at[rows_of(first, 2)], b2r[j].at[side], device)
        elif name == "b3":
            arrive("b2p", j)
            arrive("b2m", j)

            def total(q):
                at = rows_of(q, 1)
                return partial(j, 2 * here(x) + q, 1) + (
                    b2r[j][0, at].astype(F32) + b2r[j][1, at].astype(F32))
            give = rows_of(2 * here(x) + 1 - yl, 1)
            sib[j][give] = total(1 - yl).astype(BF16)
            send("b3", j, sib[j].at[give], b3r[j], low)
            own_of(j)[rows_of(2 * here(x) + yl, 1)] = total(yl)
        elif name == "fin":
            if "b" not in done:
                arrive("ob2", 1)
                done["b"] = True
            arrive("b3", j)
            value = (own_of(j)[rows_of(2 * here(x) + yl, 1)] + b3r[j][...].astype(F32)
                     + ob2r[:, columns].astype(F32)).astype(BF16)
            rows[j][own_c] = value
            send("t1", j, rows[j].at[own_c], t1r[j], out_z, moves)
            send("c1", j, rows[j].at[own_c], rows[j].at[own_c], low)

            @pl.when(jnp.logical_not(moves))
            def _():
                t1r[j][...] = value
        elif name == "c2":
            arrive("c1", j)
            pair_out("c2", j, rows[j], 8 * k, here(x), xp, xm)
        elif name == "c3":
            arrive("c2p", j)
            arrive("c2m", j)
            pass_on("c3", j, rows[j], 8 * k, here(x + 3), here(x + 1), yl, xp, xm)
        elif name == "c4":
            arrive("c3p", j)
            arrive("c3m", j)
            mine = rows[j].at[rows_of(8 * k, 8)]
            send("c4", j, mine, mine, other)
        elif name == "t2":
            arrive("t1", j)
            at = rows_of(2 * z + yl, 1)
            send("t2", j, t1r[j], cols[j].at[at], mirror, mirrored)

            @pl.when(jnp.logical_not(mirrored))
            def _():
                cols[j][at] = t1r[j][...]
        elif name == "d1":
            arrive("t2", j)
            send("d1", j, cols[j].at[own_a], cols[j].at[own_a], high)
        elif name == "d2":
            arrive("d1", j)
            pair_out("d2", j, cols[j], 0, z, zp, zm)
        elif name == "d3":
            arrive("d2p", j)
            arrive("d2m", j)
            pass_on("d3", j, cols[j], 0, (z + 3) % 4, (z + 1) % 4, yh, zp, zm)
        elif name == "w":
            arrive("d3p", j)
            arrive("d3m", j)
            arrive("c4", j)
        elif name[0] == "g":
            product(j, int(name[1]))

    for name, j in ORDER:
        run(name, j)
    for name, j in list(sent):
        leave(name, j)


def update(amplitudes, cholesky, occ_map, vir_map):
    height, width = amplitudes.shape
    s, naux = cholesky.shape
    half = 8 * s
    n = len(WIDTHS)
    many = n * len(COPIES) + 2
    lines = occ_map.shape[0] // 128

    def each(*lead):
        return [pltpu.VMEM((*lead, w), BF16) for w in WIDTHS]

    vmem = pl.BlockSpec(memory_space=pltpu.VMEM)
    return pl.pallas_call(
        kernel,
        out_shape=pltpu.VMEM((height, width), BF16),
        in_specs=[pl.BlockSpec(memory_space=pl.ANY), vmem, vmem, vmem],
        out_specs=vmem,
        scratch_shapes=[
            each(8 * s),
            [pltpu.VMEM((half, max(WIDTHS)), BF16) for _ in range(SEND_SLOTS)],
            [pltpu.VMEM((half, max(WIDTHS)), F32) for _ in range(OWN_SLOTS)],
            each(half),
            each(2, s),
            each(2, 2 * s),
            each(s),
            each(2 * half),
            each(8 * s),
            each(s),
            pltpu.VMEM((s, naux), BF16),
            pltpu.VMEM((s, naux), BF16),
            pltpu.VMEM((height, width), F32),
            pltpu.VMEM((lines, 128), F32),
            pltpu.VMEM((height, 128), F32),
            pltpu.SemaphoreType.DMA((many,)),
            pltpu.SemaphoreType.DMA((many,)),
            pltpu.SemaphoreType.DMA((1,)),
        ],
        compiler_params=pltpu.CompilerParams(
            collective_id=0, has_side_effects=True, vmem_limit_bytes=53 * 2**20),
        cost_estimate=pl.CostEstimate(
            flops=4 * height * width * naux, bytes_accessed=4 * height * width, transcendentals=0),
    )(amplitudes, cholesky, occ_map.reshape(lines, 128), vir_map.reshape(lines, 128))


def solution(mesh):
    return jax.shard_map(
        update,
        mesh=mesh,
        in_specs=(P("col", "row"), P(("row", "col"), None), P(), P()),
        out_specs=P("col", "row"),
        check_vma=False,
    )
```

```python
import jax
import jax.numpy as jnp
from jax import lax
from jax.experimental import pallas as pl
from jax.experimental.pallas import tpu as pltpu
from jax.sharding import PartitionSpec as P

NOCC = 48
NVIR = 512
MESH = pl.DeviceIdType.MESH
BF16 = jnp.bfloat16
F32 = jnp.float32

WIDTHS = [128, 256, 256, 256, 256, 128]
OWN_SLOTS = 3
SEND_SLOTS = 2
GPARTS = 2
GTILE = 256
ORDER = [
    ("a1", 0), ("a1", 2), ("a1", 3), ("a1", 1), ("a2", 0), ("a1", 4), ("a1", 5), ("a2", 2),
    ("a3", 0), ("a2", 1), ("a3", 2), ("m1", 0), ("m2", 0), ("b1", 0), ("a3", 1), ("a2", 3),
    ("a2", 5), ("m1", 2), ("b2", 0), ("m2", 2), ("m1", 1), ("b1", 2), ("m2", 1), ("b1", 1),
    ("b3", 0), ("a3", 3), ("a2", 4), ("b2", 2), ("m1", 3), ("fin", 0), ("a3", 5), ("b2", 1),
    ("m2", 3), ("b3", 2), ("b1", 3), ("gap", 0), ("t2", 0), ("c2", 0), ("a3", 4), ("m1", 5),
    ("b3", 1), ("fin", 2), ("b2", 3), ("d1", 0), ("m2", 5), ("fin", 1), ("c3", 0), ("m1", 4),
    ("m2", 4), ("b1", 5), ("b1", 4), ("d2", 0), ("t2", 2), ("t2", 1), ("b3", 3), ("d3", 0),
    ("b2", 5), ("d1", 2), ("fin", 3), ("b2", 4), ("c2", 2), ("c4", 0), ("b3", 5), ("fin", 5),
    ("b3", 4), ("d1", 1), ("d2", 2), ("c2", 1), ("t2", 3), ("fin", 4), ("t2", 5), ("d2", 1),
    ("c3", 1), ("t2", 4), ("c3", 2), ("w", 0), ("c2", 3), ("d1", 3), ("d3", 2), ("g0", 0),
    ("c2", 4), ("d3", 1), ("d1", 5), ("c4", 1), ("g1", 0), ("d1", 4), ("d2", 3), ("c4", 2),
    ("d2", 4), ("w", 1), ("w", 2), ("c3", 3), ("c2", 5), ("g0", 1), ("g0", 2), ("d3", 3),
    ("d2", 5), ("g1", 1), ("c3", 4), ("c4", 3), ("d3", 4), ("g1", 2), ("w", 3), ("c3", 5),
    ("g0", 3), ("d3", 5), ("c4", 4), ("g1", 3), ("c4", 5), ("w", 4), ("g1", 4), ("w", 5),
    ("g0", 4), ("g0", 5), ("g1", 5),
]

COPIES = [
    "a1", "a2p", "a2m", "a3p", "a3m", "dd", "b1p", "b1m", "b2p", "b2m", "b3",
    "c1", "c2p", "c2m", "c3p", "c3m", "c4", "t1", "t2", "d1", "d2p", "d2m", "d3p", "d3m",
]


def place(x, yl, k, z, yh):
    return x * 4 + yl * 2 + k, z * 2 + yh


def kernel(t_hbm, b_own, occ, vir, out, bg, p_send, p_own, sib, b1r, b2r, b3r, rows, cols, t1r,
           acc, gap, gap_rows, send_sem, recv_sem, local_sem):
    r, c = lax.axis_index("row"), lax.axis_index("col")
    x, yl, k = r // 4, (r // 2) % 2, r % 2
    z, yh = c // 2, c % 2
    n = len(WIDTHS)
    begin = [sum(WIDTHS[:j]) for j in range(n)]
    s = b_own.shape[0]
    half = 8 * s

    xp, xm = place((x + 1) % 4, yl, k, z, yh), place((x + 3) % 4, yl, k, z, yh)
    zp, zm = place(x, yl, k, (z + 1) % 4, yh), place(x, yl, k, (z + 3) % 4, yh)
    low, high = place(x, 1 - yl, k, z, yh), place(x, yl, k, z, 1 - yh)
    other = place(x, yl, 1 - k, z, yh)
    out_z, in_z = place(x, yl, k, (z + x) % 4, yh), place(x, yl, k, (z + 4 - x) % 4, yh)
    mirror_x = (z + 4 - x) % 4
    mirror = place(mirror_x, yh, k, z, yl)
    moves = x != 0
    mirrored = jnp.logical_or(mirror_x != x, yh != yl)

    barrier = pltpu.get_barrier_semaphore()
    for device in (xp, xm, zp, zm, low, high, other):
        pl.semaphore_signal(barrier, inc=1, device_id=device, device_id_type=MESH)

    @pl.when(moves)
    def _():
        pl.semaphore_signal(barrier, inc=1, device_id=in_z, device_id_type=MESH)

    @pl.when(mirrored)
    def _():
        pl.semaphore_signal(barrier, inc=1, device_id=mirror, device_id_type=MESH)

    t_copy = pltpu.make_async_copy(t_hbm, out, local_sem.at[0])
    t_copy.start()

    pl.semaphore_wait(barrier, 7 + moves.astype(jnp.int32) + mirrored.astype(jnp.int32))

    def copy(name, j, src, dst, device):
        at = j * len(COPIES) + COPIES.index(name)
        return pltpu.make_async_remote_copy(
            src_ref=src, dst_ref=dst, send_sem=send_sem.at[at], recv_sem=recv_sem.at[at],
            device_id=device, device_id_type=MESH,
        )

    def rows_of(block, count):
        return pl.ds(pl.multiple_of(block * s, s), count * s)

    def here(pos):
        return (pos + z) % 4

    sent = {}
    waiting = {}

    def send(name, j, src, dst, device, when=None):
        one = copy(name, j, src, dst, device)
        if when is None:
            one.start()
        else:
            pl.when(when)(one.start)
        sent[name, j] = waiting[name, j] = (one, when)

    def arrive(name, j):
        one, when = waiting.pop((name, j))
        if when is None:
            one.wait_recv()
        else:
            pl.when(when)(one.wait_recv)

    def leave(name, j):
        one, when = sent.pop((name, j))
        if when is None:
            one.wait_send()
        else:
            pl.when(when)(one.wait_send)

    def pair_out(name, j, buf, at, p, plus, minus):
        view = buf.at[rows_of(at + 2 * p, 2)]
        send(name + "p", j, view, view, plus)
        send(name + "m", j, view, view, minus)

    def pass_on(name, j, buf, at, before, after, q, plus, minus):
        up = buf.at[rows_of(at + 2 * before + q, 1)]
        down = buf.at[rows_of(at + 2 * after + 1 - q, 1)]
        send(name + "p", j, up, up, plus)
        send(name + "m", j, down, down, minus)

    def dressed_part(j, start):
        t = out[pl.ds(pl.multiple_of(start, half), half), :]
        return jnp.dot(t, bg[j][...], preferred_element_type=F32)

    def own_of(j):
        return p_own[j % OWN_SLOTS].at[:, pl.ds(0, WIDTHS[j])]

    def partial(j, block, count):
        at = rows_of(block, count)
        return own_of(j)[at] + sib[j][at].astype(F32)

    def set_gaps():
        gap[...] = 0.5 + 2.5 * jnp.sqrt(vir[...].astype(F32) / NVIR) + (
            0.5 + 2.5 * occ[...].astype(F32) / NOCC)
        blocks = 2 * half // 128

        def turn(i, carry):
            line = gap[pl.ds(c * blocks + i, 1), :]
            gap_rows[pl.ds(pl.multiple_of(i * 128, 128), 128), :] = jnp.broadcast_to(line, (128, 128)).T
            return carry
        lax.fori_loop(0, blocks, turn, 0)

    def product(j, part):
        tiles = acc.shape[0] // GPARTS

        def step(i, carry):
            down = pl.ds(pl.multiple_of(i * half, half), half)
            left = rows[j][down, :]
            for h in range(part * tiles, (part + 1) * tiles):
                at = h * GTILE
                value = lax.dot_general(
                    left, cols[j][at:at + GTILE, :],
                    (((1,), (1,)), ((), ())), preferred_element_type=F32)
                if j == 0:
                    acc[h, down] = value
                elif j < n - 1:
                    acc[h, down] += value
                else:
                    value = acc[h, down] + value
                    for lane in range(0, GTILE, 128):
                        line = gap[pl.ds(r * (half // 128) + (at + lane) // 128, 1), :]
                        both = gap_rows[down, :] + line
                        out[down, at + lane:at + lane + 128] = (
                            -value[:, lane:lane + 128] / both).astype(BF16)
            return carry
        lax.fori_loop(0, 2, step, 0)

    done = {}

    def run(name, j):
        own_a = rows_of(2 * z + yh, 1)
        own_c = rows_of(8 * k + 2 * here(x) + yl, 1)
        w = WIDTHS[j]
        columns = pl.ds(begin[j], w)
        if name == "gap":
            set_gaps()
        elif name == "a1":
            send("a1", j, b_own.at[:, columns], bg[j].at[own_a], high)
            bg[j][own_a] = b_own[:, columns]
        elif name == "a2":
            arrive("a1", j)
            pair_out("a2", j, bg[j], 0, z, zp, zm)
        elif name == "a3":
            arrive("a2p", j)
            arrive("a2m", j)
            pass_on("a3", j, bg[j], 0, (z + 3) % 4, (z + 1) % 4, yh, zp, zm)
        elif name == "m1":
            arrive("a3p", j)
            arrive("a3m", j)
            if "t" not in done:
                t_copy.wait()
                done["t"] = True
            if j >= SEND_SLOTS:
                leave("dd", j - SEND_SLOTS)
            slot = p_send[j % SEND_SLOTS].at[:, pl.ds(0, w)]
            slot[...] = dressed_part(j, (1 - k) * half).astype(BF16)
            send("dd", j, slot, sib[j], other)
        elif name == "m2":
            own_of(j)[...] = dressed_part(j, k * half)

            @pl.when(jnp.logical_and(x == z, yl == yh))
            def _():
                own_of(j)[...] += bg[j][...].astype(F32)
        elif name == "b1":
            arrive("dd", j)
            for side, (q, device) in enumerate(((yl, xp), (1 - yl, xm))):
                block = 2 * here(x + 2) + q
                sib[j][rows_of(block, 1)] = partial(j, block, 1).astype(BF16)
                send("b1" + "pm"[side], j, sib[j].at[rows_of(block, 1)], b1r[j].at[side], device)
        elif name == "b2":
            arrive("b1p", j)
            arrive("b1m", j)
            for side, (step, q, device) in enumerate(((1, yl, xp), (3, 1 - yl, xm))):
                first = 2 * here(x + step)
                one, two = rows_of(first + q, 1), rows_of(first + 1 - q, 1)
                sib[j][one] = (partial(j, first + q, 1) + b1r[j][side].astype(F32)).astype(BF16)
                sib[j][two] = partial(j, first + 1 - q, 1).astype(BF16)
                send("b2" + "pm"[side], j, sib[j].at[rows_of(first, 2)], b2r[j].at[side], device)
        elif name == "b3":
            arrive("b2p", j)
            arrive("b2m", j)

            def total(q):
                at = rows_of(q, 1)
                return partial(j, 2 * here(x) + q, 1) + (
                    b2r[j][0, at].astype(F32) + b2r[j][1, at].astype(F32))
            give = rows_of(2 * here(x) + 1 - yl, 1)
            sib[j][give] = total(1 - yl).astype(BF16)
            send("b3", j, sib[j].at[give], b3r[j], low)
            own_of(j)[rows_of(2 * here(x) + yl, 1)] = total(yl)
        elif name == "fin":
            arrive("b3", j)
            kept = own_of(j)[rows_of(2 * here(x) + yl, 1)]
            value = (kept + b3r[j][...].astype(F32)).astype(BF16)
            rows[j][own_c] = value
            send("t1", j, rows[j].at[own_c], t1r[j], out_z, moves)
            send("c1", j, rows[j].at[own_c], rows[j].at[own_c], low)

            @pl.when(jnp.logical_not(moves))
            def _():
                t1r[j][...] = value
        elif name == "c2":
            arrive("c1", j)
            pair_out("c2", j, rows[j], 8 * k, here(x), xp, xm)
        elif name == "c3":
            arrive("c2p", j)
            arrive("c2m", j)
            pass_on("c3", j, rows[j], 8 * k, here(x + 3), here(x + 1), yl, xp, xm)
        elif name == "c4":
            arrive("c3p", j)
            arrive("c3m", j)
            mine = rows[j].at[rows_of(8 * k, 8)]
            send("c4", j, mine, mine, other)
        elif name == "t2":
            arrive("t1", j)
            at = rows_of(2 * z + yl, 1)
            send("t2", j, t1r[j], cols[j].at[at], mirror, mirrored)

            @pl.when(jnp.logical_not(mirrored))
            def _():
                cols[j][at] = t1r[j][...]
        elif name == "d1":
            arrive("t2", j)
            send("d1", j, cols[j].at[own_a], cols[j].at[own_a], high)
        elif name == "d2":
            arrive("d1", j)
            pair_out("d2", j, cols[j], 0, z, zp, zm)
        elif name == "d3":
            arrive("d2p", j)
            arrive("d2m", j)
            pass_on("d3", j, cols[j], 0, (z + 3) % 4, (z + 1) % 4, yh, zp, zm)
        elif name == "w":
            arrive("d3p", j)
            arrive("d3m", j)
            arrive("c4", j)
        elif name[0] == "g":
            product(j, int(name[1]))

    for name, j in ORDER:
        run(name, j)
    for name, j in list(sent):
        leave(name, j)


def update(amplitudes, cholesky, occ_map, vir_map):
    height, width = amplitudes.shape
    s, naux = cholesky.shape
    half = 8 * s
    n = len(WIDTHS)
    many = n * len(COPIES)
    lines = occ_map.shape[0] // 128

    def each(*lead):
        return [pltpu.VMEM((*lead, w), BF16) for w in WIDTHS]

    vmem = pl.BlockSpec(memory_space=pltpu.VMEM)
    return pl.pallas_call(
        kernel,
        out_shape=pltpu.VMEM((height, width), BF16),
        in_specs=[pl.BlockSpec(memory_space=pl.ANY), vmem, vmem, vmem],
        out_specs=vmem,
        scratch_shapes=[
            each(8 * s),
            [pltpu.VMEM((half, max(WIDTHS)), BF16) for _ in range(SEND_SLOTS)],
            [pltpu.VMEM((half, max(WIDTHS)), F32) for _ in range(OWN_SLOTS)],
            each(half),
            each(2, s),
            each(2, 2 * s),
            each(s),
            each(2 * half),
            each(8 * s),
            each(s),
            pltpu.VMEM((width // GTILE, height, GTILE), F32),
            pltpu.VMEM((lines, 128), F32),
            pltpu.VMEM((height, 128), F32),
            pltpu.SemaphoreType.DMA((many,)),
            pltpu.SemaphoreType.DMA((many,)),
            pltpu.SemaphoreType.DMA((1,)),
        ],
        compiler_params=pltpu.CompilerParams(
            collective_id=0, has_side_effects=True, vmem_limit_bytes=53 * 2**20),
        cost_estimate=pl.CostEstimate(
            flops=4 * height * width * naux, bytes_accessed=4 * height * width, transcendentals=0),
    )(amplitudes, cholesky, occ_map.reshape(lines, 128), vir_map.reshape(lines, 128))


def solution(mesh):
    return jax.shard_map(
        update,
        mesh=mesh,
        in_specs=(P("col", "row"), P(("row", "col"), None), P(), P()),
        out_specs=P("col", "row"),
        check_vma=False,
    )
```

```python
import jax
import jax.numpy as jnp
from jax import lax
from jax.experimental import pallas as pl
from jax.experimental.pallas import tpu as pltpu
from jax.sharding import PartitionSpec as P

NOCC = 48
NVIR = 512
MESH = pl.DeviceIdType.MESH
BF16 = jnp.bfloat16
F32 = jnp.float32

WIDTHS = [128, 256, 256, 256, 256, 128]
A_LATE = (1, )
C_LATE = (3, 4, )
D_LATE = (4, )
OWN_SLOTS = 3
SEND_SLOTS = 2
GPARTS = 2
GTILE = 256
ORDER = [
    ("a1", 0), ("a1", 2), ("a1", 1), ("a2", 0), ("a2", 1), ("a1", 3), ("a3", 0), ("a2", 2),
    ("a3", 1), ("m1", 0), ("m2", 0), ("a1", 4), ("b1", 0), ("a1", 5), ("a3", 2), ("m1", 1),
    ("a2", 3), ("b2", 0), ("m2", 1), ("b1", 1), ("m1", 2), ("m2", 2), ("b1", 2), ("b3", 0),
    ("a3", 3), ("b2", 1), ("a2", 4), ("fin", 0), ("b2", 2), ("m1", 3), ("m2", 3), ("b1", 3),
    ("a2", 5), ("t2", 0), ("b3", 1), ("a3", 4), ("c2", 0), ("b2", 3), ("fin", 1), ("m1", 4),
    ("b3", 2), ("a3", 5), ("m2", 4), ("b1", 4), ("c3", 0), ("m1", 5), ("d1", 0), ("fin", 2),
    ("t2", 1), ("m2", 5), ("b3", 3), ("b1", 5), ("b2", 4), ("t2", 2), ("d2", 0), ("b2", 5),
    ("d1", 1), ("fin", 3), ("t2", 3), ("b3", 4), ("d2", 1), ("d1", 2), ("c2", 1), ("b3", 5),
    ("fin", 4), ("d3", 0), ("d1", 3), ("c2", 3), ("t2", 4), ("c4", 0), ("fin", 5), ("d3", 1),
    ("w", 0), ("d2", 2), ("g1", 0), ("c2", 2), ("c3", 3), ("d1", 4), ("c3", 1), ("t2", 5),
    ("c2", 4), ("d2", 3), ("gap", 0), ("g0", 0), ("c3", 2), ("c4", 1), ("d3", 2), ("c2", 5),
    ("d1", 5), ("d2", 4), ("c4", 3), ("w", 1), ("g0", 1), ("d3", 3), ("c3", 4), ("c4", 2),
    ("g1", 1), ("d3", 4), ("d2", 5), ("c3", 5), ("w", 2), ("g0", 2), ("g1", 2), ("w", 3),
    ("g1", 3), ("c4", 4), ("g0", 3), ("d3", 5), ("c4", 5), ("w", 4), ("g0", 4), ("g1", 4),
    ("w", 5), ("g1", 5), ("g0", 5),
]

COPIES = [
    "a1", "a2p", "a2m", "a3p", "a3m", "dd", "b1p", "b1m", "b2p", "b2m", "b3",
    "c1", "c2p", "c2m", "c3p", "c3m", "c4", "t1", "t2", "d1", "d2p", "d2m", "d3p", "d3m",
    "a1p", "a1m", "a1y", "a2u", "a2v", "a3y", "c1p", "c1m", "c1y", "c2u", "c2v", "c3y",
    "d1p", "d1m", "d1y", "d2u", "d2v", "d3y",
]


def place(x, yl, k, z, yh):
    return x * 4 + yl * 2 + k, z * 2 + yh


def kernel(t_hbm, b_own, occ, vir, out, bg, p_send, p_own, sib, b1r, b2r, b3r, rows, cols, t1r,
           acc, gap, gap_rows, send_sem, recv_sem, local_sem):
    r, c = lax.axis_index("row"), lax.axis_index("col")
    x, yl, k = r // 4, (r // 2) % 2, r % 2
    z, yh = c // 2, c % 2
    n = len(WIDTHS)
    begin = [sum(WIDTHS[:j]) for j in range(n)]
    s = b_own.shape[0]
    half = 8 * s

    xp, xm = place((x + 1) % 4, yl, k, z, yh), place((x + 3) % 4, yl, k, z, yh)
    zp, zm = place(x, yl, k, (z + 1) % 4, yh), place(x, yl, k, (z + 3) % 4, yh)
    low, high = place(x, 1 - yl, k, z, yh), place(x, yl, k, z, 1 - yh)
    other = place(x, yl, 1 - k, z, yh)
    out_z, in_z = place(x, yl, k, (z + x) % 4, yh), place(x, yl, k, (z + 4 - x) % 4, yh)
    mirror_x = (z + 4 - x) % 4
    mirror = place(mirror_x, yh, k, z, yl)
    moves = x != 0
    mirrored = jnp.logical_or(mirror_x != x, yh != yl)

    barrier = pltpu.get_barrier_semaphore()
    for device in (xp, xm, zp, zm, low, high, other):
        pl.semaphore_signal(barrier, inc=1, device_id=device, device_id_type=MESH)

    @pl.when(moves)
    def _():
        pl.semaphore_signal(barrier, inc=1, device_id=in_z, device_id_type=MESH)

    @pl.when(mirrored)
    def _():
        pl.semaphore_signal(barrier, inc=1, device_id=mirror, device_id_type=MESH)

    t_copy = pltpu.make_async_copy(t_hbm, out, local_sem.at[0])
    t_copy.start()

    pl.semaphore_wait(barrier, 7 + moves.astype(jnp.int32) + mirrored.astype(jnp.int32))

    def copy(name, j, src, dst, device):
        at = j * len(COPIES) + COPIES.index(name)
        return pltpu.make_async_remote_copy(
            src_ref=src, dst_ref=dst, send_sem=send_sem.at[at], recv_sem=recv_sem.at[at],
            device_id=device, device_id_type=MESH,
        )

    def rows_of(block, count):
        return pl.ds(pl.multiple_of(block * s, s), count * s)

    def here(pos):
        return (pos + z) % 4

    sent = {}
    waiting = {}

    def send(name, j, src, dst, device, when=None):
        one = copy(name, j, src, dst, device)
        if when is None:
            one.start()
        else:
            pl.when(when)(one.start)
        sent[name, j] = waiting[name, j] = (one, when)

    def arrive(name, j):
        one, when = waiting.pop((name, j))
        if when is None:
            one.wait_recv()
        else:
            pl.when(when)(one.wait_recv)

    def leave(name, j):
        one, when = sent.pop((name, j))
        if when is None:
            one.wait_send()
        else:
            pl.when(when)(one.wait_send)

    def pair_out(name, j, buf, at, p, plus, minus):
        view = buf.at[rows_of(at + 2 * p, 2)]
        send(name + "p", j, view, view, plus)
        send(name + "m", j, view, view, minus)

    def pass_on(name, j, buf, at, before, after, q, plus, minus):
        up = buf.at[rows_of(at + 2 * before + q, 1)]
        down = buf.at[rows_of(at + 2 * after + 1 - q, 1)]
        send(name + "p", j, up, up, plus)
        send(name + "m", j, down, down, minus)

    def late_first(name, j, src, view, plus, minus, partner):
        for end, device in zip("pmy", (plus, minus, partner)):
            send(name + "1" + end, j, src, view, device)

    def late_second(name, j, buf, at, before, after, q, plus, minus, partner):
        for end, pos, shift, device, also in (("p", before, 0, plus, "u"), ("m", after, 1, minus, "v")):
            arrive(name + "1" + end, j)
            first = (at + 2 * pos + q) * s
            part = buf.at[pl.ds(pl.multiple_of(first + shift * s // 2, s // 2), s // 2)]
            send(name + "2" + end, j, part, part, device)
            whole = buf.at[pl.ds(pl.multiple_of(first, s), s)]
            send(name + "2" + also, j, whole, whole, partner)

    def late_third(name, j, buf, at, far, q, partner):
        arrive(name + "2p", j)
        arrive(name + "2m", j)
        view = buf.at[rows_of(at + 2 * far + q, 1)]
        send(name + "3y", j, view, view, partner)

    def gathered(name, j, late):
        for end in ("1y", "2u", "2v", "3y") if late else ("3p", "3m"):
            arrive(name + end, j)

    def dressed_part(j, start):
        t = out[pl.ds(pl.multiple_of(start, half), half), :]
        return jnp.dot(t, bg[j][...], preferred_element_type=F32)

    def own_of(j):
        return p_own[j % OWN_SLOTS].at[:, pl.ds(0, WIDTHS[j])]

    def partial(j, block, count):
        at = rows_of(block, count)
        return own_of(j)[at] + sib[j][at].astype(F32)

    def set_gaps():
        gap[...] = 0.5 + 2.5 * jnp.sqrt(vir[...].astype(F32) / NVIR) + (
            0.5 + 2.5 * occ[...].astype(F32) / NOCC)
        blocks = 2 * half // 128

        def turn(i, carry):
            line = gap[pl.ds(c * blocks + i, 1), :]
            gap_rows[pl.ds(pl.multiple_of(i * 128, 128), 128), :] = jnp.broadcast_to(line, (128, 128)).T
            return carry
        lax.fori_loop(0, blocks, turn, 0)

    def product(j, part):
        tiles = acc.shape[0] // GPARTS

        def step(i, carry):
            down = pl.ds(pl.multiple_of(i * half, half), half)
            left = rows[j][down, :]
            for h in range(part * tiles, (part + 1) * tiles):
                at = h * GTILE
                value = lax.dot_general(
                    left, cols[j][at:at + GTILE, :],
                    (((1,), (1,)), ((), ())), preferred_element_type=F32)
                if j == 0:
                    acc[h, down] = value
                elif j < n - 1:
                    acc[h, down] += value
                else:
                    value = acc[h, down] + value
                    for lane in range(0, GTILE, 128):
                        line = gap[pl.ds(r * (half // 128) + (at + lane) // 128, 1), :]
                        both = gap_rows[down, :] + line
                        out[down, at + lane:at + lane + 128] = (
                            -value[:, lane:lane + 128] / both).astype(BF16)
            return carry
        lax.fori_loop(0, 2, step, 0)

    done = {}

    def run(name, j):
        own_a = rows_of(2 * z + yh, 1)
        own_c = rows_of(8 * k + 2 * here(x) + yl, 1)
        w = WIDTHS[j]
        columns = pl.ds(begin[j], w)
        if name == "gap":
            set_gaps()
        elif name == "a1":
            src, view = b_own.at[:, columns], bg[j].at[own_a]
            if j in A_LATE:
                late_first("a", j, src, view, zp, zm, high)
            else:
                send("a1", j, src, view, high)
            bg[j][own_a] = b_own[:, columns]
        elif name == "a2":
            if j in A_LATE:
                late_second("a", j, bg[j], 0, (z + 3) % 4, (z + 1) % 4, yh, zp, zm, high)
            else:
                arrive("a1", j)
                pair_out("a2", j, bg[j], 0, z, zp, zm)
        elif name == "a3":
            if j in A_LATE:
                late_third("a", j, bg[j], 0, (z + 2) % 4, yh, high)
                return
            arrive("a2p", j)
            arrive("a2m", j)
            pass_on("a3", j, bg[j], 0, (z + 3) % 4, (z + 1) % 4, yh, zp, zm)
        elif name == "m1":
            gathered("a", j, j in A_LATE)
            if "t" not in done:
                t_copy.wait()
                done["t"] = True
            if j >= SEND_SLOTS:
                leave("dd", j - SEND_SLOTS)
            slot = p_send[j % SEND_SLOTS].at[:, pl.ds(0, w)]
            slot[...] = dressed_part(j, (1 - k) * half).astype(BF16)
            send("dd", j, slot, sib[j], other)
        elif name == "m2":
            own_of(j)[...] = dressed_part(j, k * half)

            @pl.when(jnp.logical_and(x == z, yl == yh))
            def _():
                own_of(j)[...] += bg[j][...].astype(F32)
        elif name == "b1":
            arrive("dd", j)
            for side, (q, device) in enumerate(((yl, xp), (1 - yl, xm))):
                block = 2 * here(x + 2) + q
                sib[j][rows_of(block, 1)] = partial(j, block, 1).astype(BF16)
                send("b1" + "pm"[side], j, sib[j].at[rows_of(block, 1)], b1r[j].at[side], device)
        elif name == "b2":
            arrive("b1p", j)
            arrive("b1m", j)
            for side, (step, q, device) in enumerate(((1, yl, xp), (3, 1 - yl, xm))):
                first = 2 * here(x + step)
                one, two = rows_of(first + q, 1), rows_of(first + 1 - q, 1)
                sib[j][one] = (partial(j, first + q, 1) + b1r[j][side].astype(F32)).astype(BF16)
                sib[j][two] = partial(j, first + 1 - q, 1).astype(BF16)
                send("b2" + "pm"[side], j, sib[j].at[rows_of(first, 2)], b2r[j].at[side], device)
        elif name == "b3":
            arrive("b2p", j)
            arrive("b2m", j)

            def total(q):
                at = rows_of(q, 1)
                return partial(j, 2 * here(x) + q, 1) + (
                    b2r[j][0, at].astype(F32) + b2r[j][1, at].astype(F32))
            give = rows_of(2 * here(x) + 1 - yl, 1)
            sib[j][give] = total(1 - yl).astype(BF16)
            send("b3", j, sib[j].at[give], b3r[j], low)
            own_of(j)[rows_of(2 * here(x) + yl, 1)] = total(yl)
        elif name == "fin":
            arrive("b3", j)
            kept = own_of(j)[rows_of(2 * here(x) + yl, 1)]
            value = (kept + b3r[j][...].astype(F32)).astype(BF16)
            rows[j][own_c] = value
            send("t1", j, rows[j].at[own_c], t1r[j], out_z, moves)
            view = rows[j].at[own_c]
            if j in C_LATE:
                late_first("c", j, view, view, xp, xm, low)
            else:
                send("c1", j, view, view, low)

            @pl.when(jnp.logical_not(moves))
            def _():
                t1r[j][...] = value
        elif name == "c2":
            if j in C_LATE:
                late_second("c", j, rows[j], 8 * k, here(x + 3), here(x + 1), yl, xp, xm, low)
            else:
                arrive("c1", j)
                pair_out("c2", j, rows[j], 8 * k, here(x), xp, xm)
        elif name == "c3":
            if j in C_LATE:
                late_third("c", j, rows[j], 8 * k, here(x + 2), yl, low)
                return
            arrive("c2p", j)
            arrive("c2m", j)
            pass_on("c3", j, rows[j], 8 * k, here(x + 3), here(x + 1), yl, xp, xm)
        elif name == "c4":
            gathered("c", j, j in C_LATE)
            mine = rows[j].at[rows_of(8 * k, 8)]
            send("c4", j, mine, mine, other)
        elif name == "t2":
            arrive("t1", j)
            at = rows_of(2 * z + yl, 1)
            send("t2", j, t1r[j], cols[j].at[at], mirror, mirrored)

            @pl.when(jnp.logical_not(mirrored))
            def _():
                cols[j][at] = t1r[j][...]
        elif name == "d1":
            arrive("t2", j)
            view = cols[j].at[own_a]
            if j in D_LATE:
                late_first("d", j, view, view, zp, zm, high)
            else:
                send("d1", j, view, view, high)
        elif name == "d2":
            if j in D_LATE:
                late_second("d", j, cols[j], 0, (z + 3) % 4, (z + 1) % 4, yh, zp, zm, high)
            else:
                arrive("d1", j)
                pair_out("d2", j, cols[j], 0, z, zp, zm)
        elif name == "d3":
            if j in D_LATE:
                late_third("d", j, cols[j], 0, (z + 2) % 4, yh, high)
                return
            arrive("d2p", j)
            arrive("d2m", j)
            pass_on("d3", j, cols[j], 0, (z + 3) % 4, (z + 1) % 4, yh, zp, zm)
        elif name == "w":
            gathered("d", j, j in D_LATE)
            arrive("c4", j)
        elif name[0] == "g":
            product(j, int(name[1]))

    for name, j in ORDER:
        run(name, j)
    for name, j in list(sent):
        leave(name, j)


def update(amplitudes, cholesky, occ_map, vir_map):
    height, width = amplitudes.shape
    s, naux = cholesky.shape
    half = 8 * s
    n = len(WIDTHS)
    many = n * len(COPIES)
    lines = occ_map.shape[0] // 128

    def each(*lead):
        return [pltpu.VMEM((*lead, w), BF16) for w in WIDTHS]

    vmem = pl.BlockSpec(memory_space=pltpu.VMEM)
    return pl.pallas_call(
        kernel,
        out_shape=pltpu.VMEM((height, width), BF16),
        in_specs=[pl.BlockSpec(memory_space=pl.ANY), vmem, vmem, vmem],
        out_specs=vmem,
        scratch_shapes=[
            each(8 * s),
            [pltpu.VMEM((half, max(WIDTHS)), BF16) for _ in range(SEND_SLOTS)],
            [pltpu.VMEM((half, max(WIDTHS)), F32) for _ in range(OWN_SLOTS)],
            each(half),
            each(2, s),
            each(2, 2 * s),
            each(s),
            each(2 * half),
            each(8 * s),
            each(s),
            pltpu.VMEM((width // GTILE, height, GTILE), F32),
            pltpu.VMEM((lines, 128), F32),
            pltpu.VMEM((height, 128), F32),
            pltpu.SemaphoreType.DMA((many,)),
            pltpu.SemaphoreType.DMA((many,)),
            pltpu.SemaphoreType.DMA((1,)),
        ],
        compiler_params=pltpu.CompilerParams(
            collective_id=0, has_side_effects=True, vmem_limit_bytes=53 * 2**20),
        cost_estimate=pl.CostEstimate(
            flops=4 * height * width * naux, bytes_accessed=4 * height * width, transcendentals=0),
    )(amplitudes, cholesky, occ_map.reshape(lines, 128), vir_map.reshape(lines, 128))


def solution(mesh):
    return jax.shard_map(
        update,
        mesh=mesh,
        in_specs=(P("col", "row"), P(("row", "col"), None), P(), P()),
        out_specs=P("col", "row"),
        check_vma=False,
    )
```

```python
import jax
import jax.numpy as jnp
from jax import lax
from jax.experimental import pallas as pl
from jax.experimental.pallas import tpu as pltpu
from jax.sharding import PartitionSpec as P

NOCC = 48
NVIR = 512
MESH = pl.DeviceIdType.MESH
BF16 = jnp.bfloat16
F32 = jnp.float32

WIDTHS = [128, 256, 256, 256, 256, 128]
A_LATE = (1, )
C_LATE = (2, 4, )
D_LATE = (4, )
OWN_SLOTS = 3
SEND_SLOTS = 2
GPARTS = 2
GTILE = 256
ORDER = [
    ("a1", 0), ("a1", 1), ("a1", 2), ("a2", 0), ("a1", 3), ("a2", 1), ("a3", 0), ("a2", 2),
    ("a3", 1), ("m1", 0), ("m2", 0), ("a1", 4), ("b1", 0), ("a3", 2), ("a2", 3), ("m1", 1),
    ("m2", 1), ("b2", 0), ("b1", 1), ("a2", 4), ("m1", 2), ("m2", 2), ("b1", 2), ("b3", 0),
    ("a1", 5), ("a3", 3), ("b2", 1), ("b2", 2), ("a3", 4), ("fin", 0), ("m1", 3), ("a2", 5),
    ("m2", 3), ("b3", 1), ("b1", 3), ("t2", 0), ("c2", 0), ("m1", 4), ("b3", 2), ("b2", 3),
    ("fin", 1), ("m2", 4), ("d1", 0), ("b1", 4), ("fin", 2), ("t2", 1), ("a3", 5), ("d2", 0),
    ("t2", 2), ("b3", 3), ("m1", 5), ("m2", 5), ("b1", 5), ("fin", 3), ("d1", 1), ("c3", 0),
    ("b2", 4), ("d1", 2), ("b2", 5), ("d3", 0), ("c4", 0), ("t2", 3), ("c2", 1), ("c2", 2),
    ("d2", 1), ("d2", 2), ("w", 0), ("b3", 4), ("g0", 0), ("d1", 3), ("b3", 5), ("fin", 4),
    ("d3", 1), ("c3", 1), ("fin", 5), ("c3", 2), ("d2", 3), ("d3", 2), ("t2", 4), ("c2", 4),
    ("c2", 3), ("g1", 0), ("c4", 1), ("gap", 0), ("t2", 5), ("c4", 2), ("d1", 4), ("w", 1),
    ("c3", 4), ("g0", 1), ("c2", 5), ("g1", 1), ("d3", 3), ("c3", 3), ("w", 2), ("d1", 5),
    ("d2", 4), ("g0", 2), ("g1", 2), ("c4", 3), ("c4", 4), ("d2", 5), ("d3", 4), ("c3", 5),
    ("w", 3), ("g0", 3), ("g1", 3), ("c4", 5), ("d3", 5), ("w", 4), ("g0", 4), ("g1", 4),
    ("w", 5), ("g0", 5), ("g1", 5),
]

COPIES = [
    "a1", "a2p", "a2m", "a3p", "a3m", "dd", "b1p", "b1m", "b2p", "b2m", "b3",
    "c1", "c2p", "c2m", "c3p", "c3m", "c4", "t1", "t2", "d1", "d2p", "d2m", "d3p", "d3m",
    "a1p", "a1m", "a1y", "a2u", "a2v", "a3y", "c1p", "c1m", "c1y", "c2u", "c2v", "c3y",
    "d1p", "d1m", "d1y", "d2u", "d2v", "d3y",
]


def place(x, yl, k, z, yh):
    return x * 4 + yl * 2 + k, z * 2 + yh


def kernel(t_hbm, b_own, occ, vir, out, bg, p_send, p_own, sib, b1r, b2r, b3r, rows, cols, t1r,
           acc, gap, gap_rows, send_sem, recv_sem, local_sem):
    r, c = lax.axis_index("row"), lax.axis_index("col")
    x, yl, k = r // 4, (r // 2) % 2, r % 2
    z, yh = c // 2, c % 2
    n = len(WIDTHS)
    begin = [sum(WIDTHS[:j]) for j in range(n)]
    s = b_own.shape[0]
    half = 8 * s

    xp, xm = place((x + 1) % 4, yl, k, z, yh), place((x + 3) % 4, yl, k, z, yh)
    zp, zm = place(x, yl, k, (z + 1) % 4, yh), place(x, yl, k, (z + 3) % 4, yh)
    low, high = place(x, 1 - yl, k, z, yh), place(x, yl, k, z, 1 - yh)
    other = place(x, yl, 1 - k, z, yh)
    out_z, in_z = place(x, yl, k, (z + x) % 4, yh), place(x, yl, k, (z + 4 - x) % 4, yh)
    mirror_x = (z + 4 - x) % 4
    mirror = place(mirror_x, yh, k, z, yl)
    moves = x != 0
    mirrored = jnp.logical_or(mirror_x != x, yh != yl)

    barrier = pltpu.get_barrier_semaphore()
    for device in (xp, xm, zp, zm, low, high, other):
        pl.semaphore_signal(barrier, inc=1, device_id=device, device_id_type=MESH)

    @pl.when(moves)
    def _():
        pl.semaphore_signal(barrier, inc=1, device_id=in_z, device_id_type=MESH)

    @pl.when(mirrored)
    def _():
        pl.semaphore_signal(barrier, inc=1, device_id=mirror, device_id_type=MESH)

    t_copy = pltpu.make_async_copy(t_hbm, out, local_sem.at[0])
    t_copy.start()

    pl.semaphore_wait(barrier, 7 + moves.astype(jnp.int32) + mirrored.astype(jnp.int32))

    def copy(name, j, src, dst, device):
        at = j * len(COPIES) + COPIES.index(name)
        return pltpu.make_async_remote_copy(
            src_ref=src, dst_ref=dst, send_sem=send_sem.at[at], recv_sem=recv_sem.at[at],
            device_id=device, device_id_type=MESH,
        )

    def rows_of(block, count):
        return pl.ds(pl.multiple_of(block * s, s), count * s)

    def here(pos):
        return (pos + z) % 4

    sent = {}
    waiting = {}

    def send(name, j, src, dst, device, when=None):
        one = copy(name, j, src, dst, device)
        if when is None:
            one.start()
        else:
            pl.when(when)(one.start)
        sent[name, j] = waiting[name, j] = (one, when)

    def arrive(name, j):
        one, when = waiting.pop((name, j))
        if when is None:
            one.wait_recv()
        else:
            pl.when(when)(one.wait_recv)

    def leave(name, j):
        one, when = sent.pop((name, j))
        if when is None:
            one.wait_send()
        else:
            pl.when(when)(one.wait_send)

    def pair_out(name, j, buf, at, p, plus, minus):
        view = buf.at[rows_of(at + 2 * p, 2)]
        send(name + "p", j, view, view, plus)
        send(name + "m", j, view, view, minus)

    def pass_on(name, j, buf, at, before, after, q, plus, minus):
        up = buf.at[rows_of(at + 2 * before + q, 1)]
        down = buf.at[rows_of(at + 2 * after + 1 - q, 1)]
        send(name + "p", j, up, up, plus)
        send(name + "m", j, down, down, minus)

    def late_first(name, j, src, view, plus, minus, partner):
        for end, device in zip("pmy", (plus, minus, partner)):
            send(name + "1" + end, j, src, view, device)

    def late_second(name, j, buf, at, before, after, q, plus, minus, partner):
        for end, pos, shift, device, also in (("p", before, 0, plus, "u"), ("m", after, 1, minus, "v")):
            arrive(name + "1" + end, j)
            first = (at + 2 * pos + q) * s
            part = buf.at[pl.ds(pl.multiple_of(first + shift * s // 2, s // 2), s // 2)]
            send(name + "2" + end, j, part, part, device)
            whole = buf.at[pl.ds(pl.multiple_of(first, s), s)]
            send(name + "2" + also, j, whole, whole, partner)

    def late_third(name, j, buf, at, far, q, partner):
        arrive(name + "2p", j)
        arrive(name + "2m", j)
        view = buf.at[rows_of(at + 2 * far + q, 1)]
        send(name + "3y", j, view, view, partner)

    def gathered(name, j, late):
        for end in ("1y", "2u", "2v", "3y") if late else ("3p", "3m"):
            arrive(name + end, j)

    def dressed_part(j, start):
        t = out[pl.ds(pl.multiple_of(start, half), half), :]
        return jnp.dot(t, bg[j][...], preferred_element_type=F32)

    def own_of(j):
        return p_own[j % OWN_SLOTS].at[:, pl.ds(0, WIDTHS[j])]

    def partial(j, block, count):
        at = rows_of(block, count)
        return own_of(j)[at] + sib[j][at].astype(F32)

    def set_gaps():
        gap[...] = 0.5 + 2.5 * jnp.sqrt(vir[...].astype(F32) / NVIR) + (
            0.5 + 2.5 * occ[...].astype(F32) / NOCC)
        blocks = 2 * half // 128

        def turn(i, carry):
            line = gap[pl.ds(c * blocks + i, 1), :]
            gap_rows[pl.ds(pl.multiple_of(i * 128, 128), 128), :] = jnp.broadcast_to(line, (128, 128)).T
            return carry
        lax.fori_loop(0, blocks, turn, 0)

    def product(j, part):
        tiles = acc.shape[0] // GPARTS

        def step(i, carry):
            down = pl.ds(pl.multiple_of(i * half, half), half)
            left = rows[j][down, :]
            for h in range(part * tiles, (part + 1) * tiles):
                at = h * GTILE
                value = lax.dot_general(
                    left, cols[j][at:at + GTILE, :],
                    (((1,), (1,)), ((), ())), preferred_element_type=F32)
                if j == 0:
                    acc[h, down] = value
                elif j < n - 1:
                    acc[h, down] += value
                else:
                    value = acc[h, down] + value
                    for lane in range(0, GTILE, 128):
                        line = gap[pl.ds(r * (half // 128) + (at + lane) // 128, 1), :]
                        both = gap_rows[down, :] + line
                        out[down, at + lane:at + lane + 128] = (
                            -value[:, lane:lane + 128] / both).astype(BF16)
            return carry
        lax.fori_loop(0, 2, step, 0)

    done = {}

    def run(name, j):
        own_a = rows_of(2 * z + yh, 1)
        own_c = rows_of(8 * k + 2 * here(x) + yl, 1)
        w = WIDTHS[j]
        columns = pl.ds(begin[j], w)
        if name == "gap":
            set_gaps()
        elif name == "a1":
            src, view = b_own.at[:, columns], bg[j].at[own_a]
            if j in A_LATE:
                late_first("a", j, src, view, zp, zm, high)
            else:
                send("a1", j, src, view, high)
            bg[j][own_a] = b_own[:, columns]
        elif name == "a2":
            if j in A_LATE:
                late_second("a", j, bg[j], 0, (z + 3) % 4, (z + 1) % 4, yh, zp, zm, high)
            else:
                arrive("a1", j)
                pair_out("a2", j, bg[j], 0, z, zp, zm)
        elif name == "a3":
            if j in A_LATE:
                late_third("a", j, bg[j], 0, (z + 2) % 4, yh, high)
                return
            arrive("a2p", j)
            arrive("a2m", j)
            pass_on("a3", j, bg[j], 0, (z + 3) % 4, (z + 1) % 4, yh, zp, zm)
        elif name == "m1":
            gathered("a", j, j in A_LATE)
            if "t" not in done:
                t_copy.wait()
                done["t"] = True
            if j >= SEND_SLOTS:
                leave("dd", j - SEND_SLOTS)
            slot = p_send[j % SEND_SLOTS].at[:, pl.ds(0, w)]
            slot[...] = dressed_part(j, (1 - k) * half).astype(BF16)
            send("dd", j, slot, sib[j], other)
        elif name == "m2":
            own_of(j)[...] = dressed_part(j, k * half)

            @pl.when(jnp.logical_and(x == z, yl == yh))
            def _():
                own_of(j)[...] += bg[j][...].astype(F32)
        elif name == "b1":
            arrive("dd", j)
            for side, (q, device) in enumerate(((yl, xp), (1 - yl, xm))):
                block = 2 * here(x + 2) + q
                sib[j][rows_of(block, 1)] = partial(j, block, 1).astype(BF16)
                send("b1" + "pm"[side], j, sib[j].at[rows_of(block, 1)], b1r[j].at[side], device)
        elif name == "b2":
            arrive("b1p", j)
            arrive("b1m", j)
            for side, (step, q, device) in enumerate(((1, yl, xp), (3, 1 - yl, xm))):
                first = 2 * here(x + step)
                one, two = rows_of(first + q, 1), rows_of(first + 1 - q, 1)
                sib[j][one] = (partial(j, first + q, 1) + b1r[j][side].astype(F32)).astype(BF16)
                sib[j][two] = partial(j, first + 1 - q, 1).astype(BF16)
                send("b2" + "pm"[side], j, sib[j].at[rows_of(first, 2)], b2r[j].at[side], device)
        elif name == "b3":
            arrive("b2p", j)
            arrive("b2m", j)

            def total(q):
                at = rows_of(q, 1)
                return partial(j, 2 * here(x) + q, 1) + (
                    b2r[j][0, at].astype(F32) + b2r[j][1, at].astype(F32))
            give = rows_of(2 * here(x) + 1 - yl, 1)
            sib[j][give] = total(1 - yl).astype(BF16)
            send("b3", j, sib[j].at[give], b3r[j], low)
            own_of(j)[rows_of(2 * here(x) + yl, 1)] = total(yl)
        elif name == "fin":
            arrive("b3", j)
            kept = own_of(j)[rows_of(2 * here(x) + yl, 1)]
            value = (kept + b3r[j][...].astype(F32)).astype(BF16)
            rows[j][own_c] = value
            send("t1", j, rows[j].at[own_c], t1r[j], out_z, moves)
            view = rows[j].at[own_c]
            if j in C_LATE:
                late_first("c", j, view, view, xp, xm, low)
            else:
                send("c1", j, view, view, low)

            @pl.when(jnp.logical_not(moves))
            def _():
                t1r[j][...] = value
        elif name == "c2":
            if j in C_LATE:
                late_second("c", j, rows[j], 8 * k, here(x + 3), here(x + 1), yl, xp, xm, low)
            else:
                arrive("c1", j)
                pair_out("c2", j, rows[j], 8 * k, here(x), xp, xm)
        elif name == "c3":
            if j in C_LATE:
                late_third("c", j, rows[j], 8 * k, here(x + 2), yl, low)
                return
            arrive("c2p", j)
            arrive("c2m", j)
            pass_on("c3", j, rows[j], 8 * k, here(x + 3), here(x + 1), yl, xp, xm)
        elif name == "c4":
            gathered("c", j, j in C_LATE)
            mine = rows[j].at[rows_of(8 * k, 8)]
            send("c4", j, mine, mine, other)
        elif name == "t2":
            arrive("t1", j)
            at = rows_of(2 * z + yl, 1)
            send("t2", j, t1r[j], cols[j].at[at], mirror, mirrored)

            @pl.when(jnp.logical_not(mirrored))
            def _():
                cols[j][at] = t1r[j][...]
        elif name == "d1":
            arrive("t2", j)
            view = cols[j].at[own_a]
            if j in D_LATE:
                late_first("d", j, view, view, zp, zm, high)
            else:
                send("d1", j, view, view, high)
        elif name == "d2":
            if j in D_LATE:
                late_second("d", j, cols[j], 0, (z + 3) % 4, (z + 1) % 4, yh, zp, zm, high)
            else:
                arrive("d1", j)
                pair_out("d2", j, cols[j], 0, z, zp, zm)
        elif name == "d3":
            if j in D_LATE:
                late_third("d", j, cols[j], 0, (z + 2) % 4, yh, high)
                return
            arrive("d2p", j)
            arrive("d2m", j)
            pass_on("d3", j, cols[j], 0, (z + 3) % 4, (z + 1) % 4, yh, zp, zm)
        elif name == "w":
            gathered("d", j, j in D_LATE)
            arrive("c4", j)
        elif name[0] == "g":
            product(j, int(name[1]))

    for name, j in ORDER:
        run(name, j)
    for name, j in list(sent):
        leave(name, j)


def update(amplitudes, cholesky, occ_map, vir_map):
    height, width = amplitudes.shape
    s, naux = cholesky.shape
    half = 8 * s
    n = len(WIDTHS)
    many = n * len(COPIES)
    lines = occ_map.shape[0] // 128

    def each(*lead):
        return [pltpu.VMEM((*lead, w), BF16) for w in WIDTHS]

    vmem = pl.BlockSpec(memory_space=pltpu.VMEM)
    return pl.pallas_call(
        kernel,
        out_shape=pltpu.VMEM((height, width), BF16),
        in_specs=[pl.BlockSpec(memory_space=pl.ANY), vmem, vmem, vmem],
        out_specs=vmem,
        scratch_shapes=[
            each(8 * s),
            [pltpu.VMEM((half, max(WIDTHS)), BF16) for _ in range(SEND_SLOTS)],
            [pltpu.VMEM((half, max(WIDTHS)), F32) for _ in range(OWN_SLOTS)],
            each(half),
            each(2, s),
            each(2, 2 * s),
            each(s),
            each(2 * half),
            each(8 * s),
            each(s),
            pltpu.VMEM((width // GTILE, height, GTILE), F32),
            pltpu.VMEM((lines, 128), F32),
            pltpu.VMEM((height, 128), F32),
            pltpu.SemaphoreType.DMA((many,)),
            pltpu.SemaphoreType.DMA((many,)),
            pltpu.SemaphoreType.DMA((1,)),
        ],
        compiler_params=pltpu.CompilerParams(
            collective_id=0, has_side_effects=True, vmem_limit_bytes=53 * 2**20),
        cost_estimate=pl.CostEstimate(
            flops=4 * height * width * naux, bytes_accessed=4 * height * width, transcendentals=0),
    )(amplitudes, cholesky, occ_map.reshape(lines, 128), vir_map.reshape(lines, 128))


def solution(mesh):
    return jax.shard_map(
        update,
        mesh=mesh,
        in_specs=(P("col", "row"), P(("row", "col"), None), P(), P()),
        out_specs=P("col", "row"),
        check_vma=False,
    )
```

```python
import jax
import jax.numpy as jnp
from jax import lax
from jax.experimental import pallas as pl
from jax.experimental.pallas import tpu as pltpu
from jax.sharding import PartitionSpec as P

NOCC = 48
NVIR = 512
MESH = pl.DeviceIdType.MESH
BF16 = jnp.bfloat16
F32 = jnp.float32

WIDTHS = [128, 256, 256, 256, 256, 128]
A_LATE = (1, )
C_LATE = (2, 3, 4, )
D_LATE = (4, )
OWN_SLOTS = 3
SEND_SLOTS = 2
GPARTS = 2
GTILE = 256
ORDER = [
    ("a1", 0), ("a1", 1), ("a1", 2), ("a2", 0), ("a2", 1), ("a3", 0), ("a1", 3), ("a2", 2),
    ("a3", 1), ("m1", 0), ("a1", 5), ("m2", 0), ("b1", 0), ("a3", 2), ("a2", 3), ("m1", 1),
    ("m2", 1), ("b1", 1), ("a1", 4), ("a2", 5), ("b2", 0), ("m1", 2), ("m2", 2), ("b1", 2),
    ("a3", 3), ("a2", 4), ("b2", 1), ("a3", 5), ("b3", 0), ("b2", 2), ("m1", 3), ("fin", 0),
    ("m2", 3), ("b3", 1), ("b1", 3), ("t2", 0), ("c2", 0), ("a3", 4), ("b3", 2), ("b2", 3),
    ("fin", 1), ("m1", 4), ("fin", 2), ("d1", 0), ("m2", 4), ("t2", 1), ("b1", 4), ("m1", 5),
    ("b3", 3), ("m2", 5), ("b1", 5), ("t2", 2), ("c2", 2), ("d1", 1), ("d2", 0), ("b2", 5),
    ("b2", 4), ("fin", 3), ("d3", 0), ("d1", 2), ("b3", 5), ("c3", 2), ("c3", 0), ("d2", 1),
    ("d2", 2), ("t2", 3), ("fin", 5), ("b3", 4), ("c2", 1), ("c2", 3), ("c4", 0), ("gap", 0),
    ("d1", 3), ("fin", 4), ("d3", 1), ("w", 0), ("g1", 0), ("d3", 2), ("c4", 2), ("c3", 1),
    ("c3", 3), ("t2", 4), ("g0", 0), ("d2", 3), ("t2", 5), ("c2", 4), ("c2", 5), ("c4", 1),
    ("w", 1), ("w", 2), ("d1", 4), ("g1", 1), ("d1", 5), ("d3", 3), ("c4", 3), ("c3", 4),
    ("g0", 1), ("d2", 4), ("c3", 5), ("g0", 2), ("d2", 5), ("w", 3), ("g1", 2), ("c4", 4),
    ("d3", 4), ("g1", 3), ("d3", 5), ("g0", 3), ("c4", 5), ("w", 4), ("g0", 4), ("w", 5),
    ("g0", 5), ("g1", 4), ("g1", 5),
]

COPIES = [
    "a1", "a2p", "a2m", "a3p", "a3m", "dd", "b1p", "b1m", "b2p", "b2m", "b3",
    "c1", "c2p", "c2m", "c3p", "c3m", "c4", "t1", "t2", "d1", "d2p", "d2m", "d3p", "d3m",
    "a1p", "a1m", "a1y", "a2u", "a2v", "a3y", "c1p", "c1m", "c1y", "c2u", "c2v", "c3y",
    "d1p", "d1m", "d1y", "d2u", "d2v", "d3y",
]


def place(x, yl, k, z, yh):
    return x * 4 + yl * 2 + k, z * 2 + yh


def kernel(t_hbm, b_own, occ, vir, out, bg, p_send, p_own, sib, b1r, b2r, b3r, rows, cols, t1r,
           acc, gap, gap_rows, send_sem, recv_sem, local_sem):
    r, c = lax.axis_index("row"), lax.axis_index("col")
    x, yl, k = r // 4, (r // 2) % 2, r % 2
    z, yh = c // 2, c % 2
    n = len(WIDTHS)
    begin = [sum(WIDTHS[:j]) for j in range(n)]
    s = b_own.shape[0]
    half = 8 * s

    xp, xm = place((x + 1) % 4, yl, k, z, yh), place((x + 3) % 4, yl, k, z, yh)
    zp, zm = place(x, yl, k, (z + 1) % 4, yh), place(x, yl, k, (z + 3) % 4, yh)
    low, high = place(x, 1 - yl, k, z, yh), place(x, yl, k, z, 1 - yh)
    other = place(x, yl, 1 - k, z, yh)
    out_z, in_z = place(x, yl, k, (z + x) % 4, yh), place(x, yl, k, (z + 4 - x) % 4, yh)
    mirror_x = (z + 4 - x) % 4
    mirror = place(mirror_x, yh, k, z, yl)
    moves = x != 0
    mirrored = jnp.logical_or(mirror_x != x, yh != yl)

    barrier = pltpu.get_barrier_semaphore()
    for device in (xp, xm, zp, zm, low, high, other):
        pl.semaphore_signal(barrier, inc=1, device_id=device, device_id_type=MESH)

    @pl.when(moves)
    def _():
        pl.semaphore_signal(barrier, inc=1, device_id=in_z, device_id_type=MESH)

    @pl.when(mirrored)
    def _():
        pl.semaphore_signal(barrier, inc=1, device_id=mirror, device_id_type=MESH)

    t_copy = pltpu.make_async_copy(t_hbm, out, local_sem.at[0])
    t_copy.start()

    pl.semaphore_wait(barrier, 7 + moves.astype(jnp.int32) + mirrored.astype(jnp.int32))

    def copy(name, j, src, dst, device):
        at = j * len(COPIES) + COPIES.index(name)
        return pltpu.make_async_remote_copy(
            src_ref=src, dst_ref=dst, send_sem=send_sem.at[at], recv_sem=recv_sem.at[at],
            device_id=device, device_id_type=MESH,
        )

    def rows_of(block, count):
        return pl.ds(pl.multiple_of(block * s, s), count * s)

    def here(pos):
        return (pos + z) % 4

    sent = {}
    waiting = {}

    def send(name, j, src, dst, device, when=None):
        one = copy(name, j, src, dst, device)
        if when is None:
            one.start()
        else:
            pl.when(when)(one.start)
        sent[name, j] = waiting[name, j] = (one, when)

    def arrive(name, j):
        one, when = waiting.pop((name, j))
        if when is None:
            one.wait_recv()
        else:
            pl.when(when)(one.wait_recv)

    def leave(name, j):
        one, when = sent.pop((name, j))
        if when is None:
            one.wait_send()
        else:
            pl.when(when)(one.wait_send)

    def pair_out(name, j, buf, at, p, plus, minus):
        view = buf.at[rows_of(at + 2 * p, 2)]
        send(name + "p", j, view, view, plus)
        send(name + "m", j, view, view, minus)

    def pass_on(name, j, buf, at, before, after, q, plus, minus):
        up = buf.at[rows_of(at + 2 * before + q, 1)]
        down = buf.at[rows_of(at + 2 * after + 1 - q, 1)]
        send(name + "p", j, up, up, plus)
        send(name + "m", j, down, down, minus)

    def late_first(name, j, src, view, plus, minus, partner):
        for end, device in zip("pmy", (plus, minus, partner)):
            send(name + "1" + end, j, src, view, device)

    def late_second(name, j, buf, at, before, after, q, plus, minus, partner):
        for end, pos, shift, device, also in (("p", before, 0, plus, "u"), ("m", after, 1, minus, "v")):
            arrive(name + "1" + end, j)
            first = (at + 2 * pos + q) * s
            part = buf.at[pl.ds(pl.multiple_of(first + shift * s // 2, s // 2), s // 2)]
            send(name + "2" + end, j, part, part, device)
            whole = buf.at[pl.ds(pl.multiple_of(first, s), s)]
            send(name + "2" + also, j, whole, whole, partner)

    def late_third(name, j, buf, at, far, q, partner):
        arrive(name + "2p", j)
        arrive(name + "2m", j)
        view = buf.at[rows_of(at + 2 * far + q, 1)]
        send(name + "3y", j, view, view, partner)

    def gathered(name, j, late):
        for end in ("1y", "2u", "2v", "3y") if late else ("3p", "3m"):
            arrive(name + end, j)

    def dressed_part(j, start):
        t = out[pl.ds(pl.multiple_of(start, half), half), :]
        return jnp.dot(t, bg[j][...], preferred_element_type=F32)

    def own_of(j):
        return p_own[j % OWN_SLOTS].at[:, pl.ds(0, WIDTHS[j])]

    def partial(j, block, count):
        at = rows_of(block, count)
        return own_of(j)[at] + sib[j][at].astype(F32)

    def set_gaps():
        gap[...] = 0.5 + 2.5 * jnp.sqrt(vir[...].astype(F32) / NVIR) + (
            0.5 + 2.5 * occ[...].astype(F32) / NOCC)
        blocks = 2 * half // 128

        def turn(i, carry):
            line = gap[pl.ds(c * blocks + i, 1), :]
            gap_rows[pl.ds(pl.multiple_of(i * 128, 128), 128), :] = jnp.broadcast_to(line, (128, 128)).T
            return carry
        lax.fori_loop(0, blocks, turn, 0)

    def product(j, part):
        tiles = acc.shape[0] // GPARTS

        def step(i, carry):
            down = pl.ds(pl.multiple_of(i * half, half), half)
            left = rows[j][down, :]
            for h in range(part * tiles, (part + 1) * tiles):
                at = h * GTILE
                value = lax.dot_general(
                    left, cols[j][at:at + GTILE, :],
                    (((1,), (1,)), ((), ())), preferred_element_type=F32)
                if j == 0:
                    acc[h, down] = value
                elif j < n - 1:
                    acc[h, down] += value
                else:
                    value = acc[h, down] + value
                    for lane in range(0, GTILE, 128):
                        line = gap[pl.ds(r * (half // 128) + (at + lane) // 128, 1), :]
                        both = gap_rows[down, :] + line
                        out[down, at + lane:at + lane + 128] = (
                            -value[:, lane:lane + 128] / both).astype(BF16)
            return carry
        lax.fori_loop(0, 2, step, 0)

    done = {}

    def run(name, j):
        own_a = rows_of(2 * z + yh, 1)
        own_c = rows_of(8 * k + 2 * here(x) + yl, 1)
        w = WIDTHS[j]
        columns = pl.ds(begin[j], w)
        if name == "gap":
            set_gaps()
        elif name == "a1":
            src, view = b_own.at[:, columns], bg[j].at[own_a]
            if j in A_LATE:
                late_first("a", j, src, view, zp, zm, high)
            else:
                send("a1", j, src, view, high)
            bg[j][own_a] = b_own[:, columns]
        elif name == "a2":
            if j in A_LATE:
                late_second("a", j, bg[j], 0, (z + 3) % 4, (z + 1) % 4, yh, zp, zm, high)
            else:
                arrive("a1", j)
                pair_out("a2", j, bg[j], 0, z, zp, zm)
        elif name == "a3":
            if j in A_LATE:
                late_third("a", j, bg[j], 0, (z + 2) % 4, yh, high)
                return
            arrive("a2p", j)
            arrive("a2m", j)
            pass_on("a3", j, bg[j], 0, (z + 3) % 4, (z + 1) % 4, yh, zp, zm)
        elif name == "m1":
            gathered("a", j, j in A_LATE)
            if "t" not in done:
                t_copy.wait()
                done["t"] = True
            if j >= SEND_SLOTS:
                leave("dd", j - SEND_SLOTS)
            slot = p_send[j % SEND_SLOTS].at[:, pl.ds(0, w)]
            slot[...] = dressed_part(j, (1 - k) * half).astype(BF16)
            send("dd", j, slot, sib[j], other)
        elif name == "m2":
            own_of(j)[...] = dressed_part(j, k * half)

            @pl.when(jnp.logical_and(x == z, yl == yh))
            def _():
                own_of(j)[...] += bg[j][...].astype(F32)
        elif name == "b1":
            arrive("dd", j)
            for side, (q, device) in enumerate(((yl, xp), (1 - yl, xm))):
                block = 2 * here(x + 2) + q
                sib[j][rows_of(block, 1)] = partial(j, block, 1).astype(BF16)
                send("b1" + "pm"[side], j, sib[j].at[rows_of(block, 1)], b1r[j].at[side], device)
        elif name == "b2":
            arrive("b1p", j)
            arrive("b1m", j)
            for side, (step, q, device) in enumerate(((1, yl, xp), (3, 1 - yl, xm))):
                first = 2 * here(x + step)
                one, two = rows_of(first + q, 1), rows_of(first + 1 - q, 1)
                sib[j][one] = (partial(j, first + q, 1) + b1r[j][side].astype(F32)).astype(BF16)
                sib[j][two] = partial(j, first + 1 - q, 1).astype(BF16)
                send("b2" + "pm"[side], j, sib[j].at[rows_of(first, 2)], b2r[j].at[side], device)
        elif name == "b3":
            arrive("b2p", j)
            arrive("b2m", j)

            def total(q):
                at = rows_of(q, 1)
                return partial(j, 2 * here(x) + q, 1) + (
                    b2r[j][0, at].astype(F32) + b2r[j][1, at].astype(F32))
            give = rows_of(2 * here(x) + 1 - yl, 1)
            sib[j][give] = total(1 - yl).astype(BF16)
            send("b3", j, sib[j].at[give], b3r[j], low)
            own_of(j)[rows_of(2 * here(x) + yl, 1)] = total(yl)
        elif name == "fin":
            arrive("b3", j)
            kept = own_of(j)[rows_of(2 * here(x) + yl, 1)]
            value = (kept + b3r[j][...].astype(F32)).astype(BF16)
            rows[j][own_c] = value
            send("t1", j, rows[j].at[own_c], t1r[j], out_z, moves)
            view = rows[j].at[own_c]
            if j in C_LATE:
                late_first("c", j, view, view, xp, xm, low)
            else:
                send("c1", j, view, view, low)

            @pl.when(jnp.logical_not(moves))
            def _():
                t1r[j][...] = value
        elif name == "c2":
            if j in C_LATE:
                late_second("c", j, rows[j], 8 * k, here(x + 3), here(x + 1), yl, xp, xm, low)
            else:
                arrive("c1", j)
                pair_out("c2", j, rows[j], 8 * k, here(x), xp, xm)
        elif name == "c3":
            if j in C_LATE:
                late_third("c", j, rows[j], 8 * k, here(x + 2), yl, low)
                return
            arrive("c2p", j)
            arrive("c2m", j)
            pass_on("c3", j, rows[j], 8 * k, here(x + 3), here(x + 1), yl, xp, xm)
        elif name == "c4":
            gathered("c", j, j in C_LATE)
            mine = rows[j].at[rows_of(8 * k, 8)]
            send("c4", j, mine, mine, other)
        elif name == "t2":
            arrive("t1", j)
            at = rows_of(2 * z + yl, 1)
            send("t2", j, t1r[j], cols[j].at[at], mirror, mirrored)

            @pl.when(jnp.logical_not(mirrored))
            def _():
                cols[j][at] = t1r[j][...]
        elif name == "d1":
            arrive("t2", j)
            view = cols[j].at[own_a]
            if j in D_LATE:
                late_first("d", j, view, view, zp, zm, high)
            else:
                send("d1", j, view, view, high)
        elif name == "d2":
            if j in D_LATE:
                late_second("d", j, cols[j], 0, (z + 3) % 4, (z + 1) % 4, yh, zp, zm, high)
            else:
                arrive("d1", j)
                pair_out("d2", j, cols[j], 0, z, zp, zm)
        elif name == "d3":
            if j in D_LATE:
                late_third("d", j, cols[j], 0, (z + 2) % 4, yh, high)
                return
            arrive("d2p", j)
            arrive("d2m", j)
            pass_on("d3", j, cols[j], 0, (z + 3) % 4, (z + 1) % 4, yh, zp, zm)
        elif name == "w":
            gathered("d", j, j in D_LATE)
            arrive("c4", j)
        elif name[0] == "g":
            product(j, int(name[1]))

    for name, j in ORDER:
        run(name, j)
    for name, j in list(sent):
        leave(name, j)


def update(amplitudes, cholesky, occ_map, vir_map):
    height, width = amplitudes.shape
    s, naux = cholesky.shape
    half = 8 * s
    n = len(WIDTHS)
    many = n * len(COPIES)
    lines = occ_map.shape[0] // 128

    def each(*lead):
        return [pltpu.VMEM((*lead, w), BF16) for w in WIDTHS]

    vmem = pl.BlockSpec(memory_space=pltpu.VMEM)
    return pl.pallas_call(
        kernel,
        out_shape=pltpu.VMEM((height, width), BF16),
        in_specs=[pl.BlockSpec(memory_space=pl.ANY), vmem, vmem, vmem],
        out_specs=vmem,
        scratch_shapes=[
            each(8 * s),
            [pltpu.VMEM((half, max(WIDTHS)), BF16) for _ in range(SEND_SLOTS)],
            [pltpu.VMEM((half, max(WIDTHS)), F32) for _ in range(OWN_SLOTS)],
            each(half),
            each(2, s),
            each(2, 2 * s),
            each(s),
            each(2 * half),
            each(8 * s),
            each(s),
            pltpu.VMEM((width // GTILE, height, GTILE), F32),
            pltpu.VMEM((lines, 128), F32),
            pltpu.VMEM((height, 128), F32),
            pltpu.SemaphoreType.DMA((many,)),
            pltpu.SemaphoreType.DMA((many,)),
            pltpu.SemaphoreType.DMA((1,)),
        ],
        compiler_params=pltpu.CompilerParams(
            collective_id=0, has_side_effects=True, vmem_limit_bytes=53 * 2**20),
        cost_estimate=pl.CostEstimate(
            flops=4 * height * width * naux, bytes_accessed=4 * height * width, transcendentals=0),
    )(amplitudes, cholesky, occ_map.reshape(lines, 128), vir_map.reshape(lines, 128))


def solution(mesh):
    return jax.shard_map(
        update,
        mesh=mesh,
        in_specs=(P("col", "row"), P(("row", "col"), None), P(), P()),
        out_specs=P("col", "row"),
        check_vma=False,
    )
```
